32 devices in a mesh: mem: 4 (over y, core), strip: 8 (over z, x).
Axes of the slice: x: 2, y: 2, z: 4, core: 2. Of those that a mesh axis runs over, the one named last changes fastest.
Arguments:
- gradient: float32 [8, 256, 1024], P('mem', 'strip'), may hold values from -6 to 6
- perturbations: bfloat16 [64, 8, 256, 1024], P('mem', None, 'strip'), may hold values from -6 to 6
- counts: int32 [256, 1024], P('strip'), may hold values from 1 to 4, as said below
Outputs:
- increment: float32 [8, 256, 1024], P('mem', 'strip')
The draws below stay inside these ranges and needn't reach their ends.
Inputs may be any that keep to these rules, and one draw needn't show every extreme that they name: `counts`: counts are drawn band by band of 32 rows along the first dimension, each band under a cap of its own; some cell reaches 4.
All inputs are finite; a program needn't handle non-finite values.
Results may differ from the reference program's by a relative error of at most 0.0003.
Values sent between devices are 32-bit elements; how exact they have to be, the bound alone decides.
No kernel may reach another device: no remote copies, remote signals or barrier semaphores. Data moves between devices by JAX's collectives and lax.ppermute only.
A program may use at most 64 MiB of HBM per device.

```python
import math
import jax
import jax.numpy as jnp
from jax import lax

SLOTS = 2
VARS = 4
FIELDS = 8
SWEEPS = 4
MEMB_DEV = 16
MEMBERS = 64
CX = 32
NY = 1024
NX = 256
N_MEM = 4


def draw_counts(key, part):
    key_caps = jax.random.fold_in(key, 11)
    key_cells = jax.random.fold_in(key, 12)
    band_count = NX // CX
    band_caps = jax.random.randint(key_caps, (band_count,), 1, SWEEPS + 1)
    band_caps = band_caps.at[0].set(SWEEPS)
    row_caps = jnp.repeat(band_caps, CX)
    raw_cells = jax.random.randint(key_cells, (NX, NY), 0, 1 << 20)
    result = 1 + raw_cells % row_caps[:, None]
    result = result.at[0, 0].set(SWEEPS)
    return result.astype(jnp.int32)


def levels(stream_key, shape, cuts, least, high):
    gain, own = 1.0, jax.random.fold_in(stream_key, 6)
    for axis_at, blocks in cuts:
        steps = jnp.exp(jax.random.uniform(jax.random.fold_in(own, axis_at), (blocks,), jnp.float32, least / len(cuts), high / len(cuts)))
        gain = gain * jnp.repeat(steps, shape[axis_at] // blocks).reshape([-1 if axis == axis_at else 1 for axis in range(len(shape))])
    return gain


def scatter_about(own_key, extent, spread, reach, split=(), kind=jnp.bfloat16):
    factor_of = levels(own_key, extent, split, -0.22, 0.18) if split else 1.0
    entries = jax.random.normal(own_key, extent, jnp.float32) * spread * factor_of
    return jnp.minimum(jnp.maximum(entries, -reach), reach).astype(kind)


def setup_inputs(seed: int = 0) -> dict:
    splits = jax.random.split(jax.random.key(seed), 4)
    gradient = scatter_about(splits[0], (FIELDS, NX, NY), 1.0, 6.0, ((0, 4), (1, 8)), jnp.float32)
    perturbations = scatter_about(splits[1], (MEMBERS, FIELDS, NX, NY), 1.0, 6.0, ((0, 4), (2, 8)))
    counts = draw_counts(jax.random.fold_in(splits[3], 71), 0)
    return {"gradient": gradient, "perturbations": perturbations, "counts": counts}


COEFF_X = 0.35
COEFF_Y = 0.12

def sweep_once(state_field, active):
    widths = ((0, 0), (0, 0), (1, 1), (1, 1))
    padded = jnp.pad(state_field, widths)
    along_x = padded[:, :, 2:, 1:-1] + padded[:, :, :-2, 1:-1] - 2.0 * state_field
    along_y = padded[:, :, 1:-1, 2:] + padded[:, :, 1:-1, :-2] - 2.0 * state_field
    return state_field + active * (COEFF_X * along_x + COEFF_Y * along_y)

def reference(gradient, perturbations, counts):
    grad_slots = gradient.reshape(SLOTS, VARS, NX, NY)
    grouped = perturbations.reshape(N_MEM, MEMB_DEV, FIELDS, NX, NY)

    def accumulate(running, member_block):
        block_values = member_block.astype(jnp.float32).reshape(MEMB_DEV, SLOTS, VARS, NX, NY)
        state_field = lax.optimization_barrier(jnp.sum(block_values * grad_slots[None], axis=2))
        for sweep_index in range(SWEEPS):
            active = (counts > sweep_index).astype(jnp.float32)
            state_field = sweep_once(state_field, active)
        member_term = lax.optimization_barrier(jnp.sum(block_values * state_field[:, :, None], axis=0))
        return (running + member_term.reshape(FIELDS, NX, NY), None)
    running, unused = lax.scan(accumulate, jnp.zeros((FIELDS, NX, NY), jnp.float32), grouped)
    return running * (1.0 / math.sqrt(MEMBERS * FIELDS))
```

```python
import math

import jax
import jax.numpy as jnp
from jax import lax
from jax.experimental import pallas as pl
from jax.experimental.pallas import tpu as pltpu
from jax.sharding import PartitionSpec as P

SLOTS = 2
VARS = 4
FIELDS = 8
SWEEPS = 4

COEFF_X = 0.35
COEFF_Y = 0.12
CENTRE = 1.0 - 2.0 * COEFF_X - 2.0 * COEFF_Y
RATIO = COEFF_Y / COEFF_X

LANES = 128
TILE = 8
HALF = 16
VMEM_BYTES = 40 * 2**20


def kernel_call(body, out_shape, scratch, flops, name):
    def call(*args):
        moved = sum(a.size * a.dtype.itemsize for a in args)
        return pl.pallas_call(
            body,
            out_shape=out_shape,
            in_specs=[pl.BlockSpec(memory_space=pltpu.VMEM)] * len(args),
            out_specs=jax.tree.map(lambda _: pl.BlockSpec(memory_space=pltpu.VMEM), out_shape),
            scratch_shapes=scratch,
            compiler_params=pltpu.CompilerParams(vmem_limit_bytes=VMEM_BYTES),
            cost_estimate=pl.CostEstimate(flops=flops, bytes_accessed=moved, transcendentals=0),
            name=name,
        )(*args)

    return call


def lane_masks():
    lane = lax.broadcasted_iota(jnp.int32, (TILE, LANES), 1)
    return lane == 0, lane == LANES - 1


def top_half():
    return lax.broadcasted_iota(jnp.int32, (TILE, LANES), 0) < TILE // 2


def cols(j):
    return pl.ds(j * LANES, LANES)


def sides(values, first, last):
    before = [pltpu.roll(v, 1, 1) for v in values]
    after = [pltpu.roll(v, LANES - 1, 1) for v in values]
    zero = jnp.zeros_like(values[0])
    count = len(values)
    sums = []
    for j in range(count):
        left = jnp.where(first, before[j - 1] if j else zero, before[j])
        right = jnp.where(last, after[j + 1] if j + 1 < count else zero, after[j])
        sums.append(left + right)
    return sums


def fields_of(local, own):
    shares = VARS // own
    mem = lax.axis_index("mem")
    slot = mem // shares
    slot = slot if local else SLOTS - 1 - slot
    share = mem % shares
    return [slot * VARS + at * own + k for at in (share, shares - 1 - share) for k in range(own)]


def project_edges(local, p_ref, ga_ref, gb_ref, *rest):
    if local:
        counts_ref, e_ref, o_ref, u_ref = rest
    else:
        e_ref, o_ref, u_ref = rest
    members, _, rows, ny = p_ref.shape
    own = ga_ref.shape[0]
    grows = ga_ref.shape[1]
    even = lax.axis_index("strip") % 2 == 0
    half = top_half()
    fields = fields_of(local, own)
    grads = [(ga_ref, k) for k in range(own)] + [(gb_ref, k) for k in range(own)]

    def put(row, j, top, bottom):
        e_ref[row, :, cols(j)] = jnp.where(even, bottom, top)
        o_ref[row, :, cols(j)] = jnp.where(even, top, bottom)

    if local:
        for j in range(ny // LANES):
            top = counts_ref[0:TILE, cols(j)].astype(jnp.float32)
            bottom = counts_ref[rows - TILE : rows, cols(j)].astype(jnp.float32)
            put(members // 2, j, top, pltpu.roll(bottom, TILE // 2, 0))

    def pair(q, carry):
        for j in range(ny // LANES):
            tops, bottoms = [], []
            for m in (2 * q, 2 * q + 1):
                top = bottom = None
                for f, (g_ref, k) in zip(fields, grads):
                    low = p_ref[m, f, 0:HALF, cols(j)].astype(jnp.float32)[0:TILE]
                    high = p_ref[m, f, rows - HALF : rows, cols(j)].astype(jnp.float32)[HALF - TILE :]
                    low = low * g_ref[k, 0:TILE, cols(j)]
                    high = high * g_ref[k, grows - TILE : grows, cols(j)]
                    top = low if top is None else top + low
                    bottom = high if bottom is None else bottom + high
                u_ref[m, 0:TILE, cols(j)] = top
                u_ref[m, TILE : 2 * TILE, cols(j)] = bottom
                tops.append(top)
                bottoms.append(bottom)
            top = jnp.where(half, tops[0], pltpu.roll(tops[1], TILE // 2, 0))
            bottom = jnp.where(half, pltpu.roll(bottoms[0], TILE // 2, 0), bottoms[1])
            put(q, j, top, bottom)
        return carry

    lax.fori_loop(0, members // 2, pair, 0)


def interior(local, p_ref, ga_ref, gb_ref, counts_ref, own_ref, other_ref, coef, buf_a, buf_b):
    members, _, rows, ny = p_ref.shape
    own = ga_ref.shape[0]
    blocks = ny // LANES
    group = buf_a.shape[0]
    first, last = lane_masks()
    fields = fields_of(local, own)
    grads = [(ga_ref, k) for k in range(own)] + [(gb_ref, k) for k in range(own)]
    sums = [(own_ref, k) for k in range(own)] + [(other_ref, k) for k in range(own)]
    for t in range(1, SWEEPS):
        for j in range(blocks):
            active = (counts_ref[:, cols(j)] > t).astype(jnp.float32)
            coef[t - 1, 0, j] = active * COEFF_X
            coef[t - 1, 1, j] = 1.0 - active * (1.0 - CENTRE)
    zero = jnp.zeros((TILE, LANES), jnp.float32)
    for buf in (buf_a, buf_b):
        for i in range(group):
            for j in range(blocks):
                buf[i, j, 0:TILE] = zero
                buf[i, j, TILE + rows :] = zero
    own_ref[...] = jnp.zeros_like(own_ref)
    other_ref[...] = jnp.zeros_like(other_ref)

    def step(s, carry):
        base = s * group
        for r in range(0, rows, HALF):
            for j in range(blocks):
                weights = [g_ref[k, r : r + HALF, cols(j)] for g_ref, k in grads]
                for i in range(group):
                    total = None
                    for f, w in zip(fields, weights):
                        term = p_ref[base + i, f, r : r + HALF, cols(j)].astype(jnp.float32) * w
                        total = term if total is None else total + term
                    buf_a[i, j, TILE + r : TILE + r + HALF] = total
        src, dst = buf_a, buf_b
        for t in range(SWEEPS):
            for r in range(0, rows, TILE):
                at = TILE + r
                for i in range(group):
                    centre = [src[i, j, at : at + TILE] for j in range(blocks)]
                    lateral = sides(centre, first, last)
                    for j in range(blocks):
                        stacked = src[i, j, at - 1 : at - 1 + TILE] + src[i, j, at + 1 : at + 1 + TILE]
                        moved = stacked + RATIO * lateral[j]
                        if t == 0:
                            new = COEFF_X * moved + CENTRE * centre[j]
                        else:
                            new = coef[t - 1, 0, j, r : r + TILE] * moved + coef[t - 1, 1, j, r : r + TILE] * centre[j]
                        dst[i, j, at : at + TILE] = new
            src, dst = dst, src
        for r in range(0, rows, HALF):
            for j in range(blocks):
                smooth = [src[i, j, TILE + r : TILE + r + HALF] for i in range(group)]
                for f, (ref, k) in zip(fields, sums):
                    total = ref[k, r : r + HALF, cols(j)]
                    for i in range(group):
                        total = total + p_ref[base + i, f, r : r + HALF, cols(j)].astype(jnp.float32) * smooth[i]
                    ref[k, r : r + HALF, cols(j)] = total
        return carry

    lax.fori_loop(0, members // group, step, 0)


def edges(local, p_ref, u_ref, e_ref, o_ref, ce_ref, co_ref, counts_ref, own_ref, other_ref, coef, buf_a, buf_b, halo):
    members, _, rows, ny = p_ref.shape
    own = own_ref.shape[0]
    blocks = ny // LANES
    first, last = lane_masks()
    half = top_half()
    even = lax.axis_index("strip") % 2 == 0
    fields = fields_of(local, own)
    sums = [(own_ref, k) for k in range(own)] + [(other_ref, k) for k in range(own)]
    crow = ce_ref.shape[0] - 1
    for j in range(blocks):
        e, o = ce_ref[crow, :, cols(j)], co_ref[crow, :, cols(j)]
        above, below = jnp.where(even, o, e), jnp.where(even, e, o)
        halo[0, j, 4:12] = above
        halo[0, j, 24:32] = below
        halo[0, j, 8:16] = counts_ref[0:TILE, cols(j)].astype(jnp.float32)
        halo[0, j, 16:24] = counts_ref[rows - TILE : rows, cols(j)].astype(jnp.float32)
        for t in range(SWEEPS):
            active = (halo[0, j, 0:32] > t).astype(jnp.float32)
            coef[t, 0, j, 0:32] = active * COEFF_X
            coef[t, 1, j, 0:32] = 1.0 - active * (1.0 - CENTRE)
        for buf in (buf_a, buf_b):
            for i in range(2):
                buf[i, j] = jnp.zeros_like(buf[i, j])
        coef[0, 0, j, 32:40] = jnp.zeros((TILE, LANES), jnp.float32)
        coef[0, 1, j, 32:40] = jnp.zeros((TILE, LANES), jnp.float32)
    own_ref[...] = jnp.zeros_like(own_ref)
    other_ref[...] = jnp.zeros_like(other_ref)
    starts = [(5, 13, 21), (6, 18), (6, 18)]

    def step(q, carry):
        for j in range(blocks):
            e, o = e_ref[q, :, cols(j)], o_ref[q, :, cols(j)]
            above, below = jnp.where(even, o, e), jnp.where(even, e, o)
            buf_a[0, j, 4:12] = above
            buf_a[0, j, 24:32] = below
            buf_a[1, j, 0:8] = above
            buf_a[1, j, 20:28] = below
            for i in range(2):
                buf_a[i, j, 8:16] = u_ref[2 * q + i, 0:TILE, cols(j)]
                buf_a[i, j, 16:24] = u_ref[2 * q + i, TILE : 2 * TILE, cols(j)]
        src, dst = buf_a, buf_b
        for t in range(SWEEPS - 1):
            for at in starts[t]:
                weights = [[coef[t, c, j, at : at + TILE] for j in range(blocks)] for c in range(2)]
                for i in range(2):
                    centre = [src[i, j, at : at + TILE] for j in range(blocks)]
                    lateral = sides(centre, first, last)
                    for j in range(blocks):
                        stacked = src[i, j, at - 1 : at - 1 + TILE] + src[i, j, at + 1 : at + 1 + TILE]
                        moved = stacked + RATIO * lateral[j]
                        dst[i, j, at : at + TILE] = weights[0][j] * moved + weights[1][j] * centre[j]
            src, dst = dst, src
        both = lambda ref, *at: jnp.where(half, ref[(*at[:-1], pl.ds(8 + at[-1], TILE))], ref[(*at[:-1], pl.ds(16 + at[-1], TILE))])
        t = SWEEPS - 1
        weights = [[both(coef, t, c, j, 0) for j in range(blocks)] for c in range(2)]
        smooth = []
        for i in range(2):
            centre = [both(src, i, j, 0) for j in range(blocks)]
            lateral = sides(centre, first, last)
            result = []
            for j in range(blocks):
                moved = both(src, i, j, -1) + both(src, i, j, 1) + RATIO * lateral[j]
                result.append(weights[0][j] * moved + weights[1][j] * centre[j])
            smooth.append(result)
        for j in range(blocks):
            for f, (ref, k) in zip(fields, sums):
                total = ref[k, :, cols(j)]
                for i in range(2):
                    low = p_ref[2 * q + i, f, 0:HALF, cols(j)].astype(jnp.float32)[0:TILE]
                    high = p_ref[2 * q + i, f, rows - HALF : rows, cols(j)].astype(jnp.float32)[HALF - TILE :]
                    total = total + jnp.where(half, low, high) * smooth[i][j]
                ref[k, :, cols(j)] = total
        return carry

    lax.fori_loop(0, members // 2, step, 0)


def finish(scale, a_ref, b_ref, c_ref, ea_ref, eb_ref, ec_ref, out_ref):
    own, rows, ny = out_ref.shape
    half = top_half()
    for k in range(own):
        for j in range(ny // LANES):
            edge = ea_ref[k, :, cols(j)] + eb_ref[k, :, cols(j)] + ec_ref[k, :, cols(j)]
            inner = a_ref[k, :, cols(j)] + b_ref[k, :, cols(j)] + c_ref[k, :, cols(j)]
            out_ref[k, 0:TILE, cols(j)] = jnp.where(half, edge, inner[0:TILE]) * scale
            out_ref[k, TILE : rows - TILE, cols(j)] = inner[TILE : rows - TILE] * scale
            out_ref[k, rows - TILE :, cols(j)] = jnp.where(half, inner[rows - TILE :], edge) * scale


def per_device(gradient, perturbations, counts):
    members, _, rows, ny = perturbations.shape
    own = gradient.shape[0]
    mem, strips = lax.axis_size("mem"), lax.axis_size("strip")
    shares = VARS // own
    blocks = ny // LANES
    assert shares == 2 and mem == shares * SLOTS and members % 2 == 0
    scale = 1.0 / math.sqrt(members * mem * FIELDS)
    f32 = jnp.float32

    near = [(i, i ^ 1) for i in range(mem)]
    across = [(i, (i + shares) % mem) for i in range(mem)]
    even = [(i, i ^ 1) for i in range(strips) if i ^ 1 < strips]
    odd = [(i, i + 1) for i in range(1, strips - 1, 2)]
    odd = odd + [(j, i) for i, j in odd]

    def shape(*dims):
        return jax.ShapeDtypeStruct(dims, f32)

    def window(*lead):
        return pltpu.VMEM((*lead, blocks, 40, LANES), f32)

    def send_shapes(extra):
        pairs = members // 2
        return (shape(pairs + extra, TILE, ny), shape(pairs + extra, TILE, ny), shape(members, 2 * TILE, ny))

    tile_flops = members * ny * 2 * VARS

    def call_edges(local):
        outs = (shape(own, TILE, ny), shape(own, TILE, ny))
        return kernel_call(
            lambda *refs: edges(local, *refs), outs,
            [window(SWEEPS, 2), window(2), window(2), window(1)],
            tile_flops * 200, "edges",
        )

    def call_interior(local):
        outs = (shape(own, rows, ny), shape(own, rows, ny))
        buf = pltpu.VMEM((2, blocks, rows + 2 * TILE, LANES), f32)
        return kernel_call(
            lambda *refs: interior(local, *refs), outs,
            [pltpu.VMEM((SWEEPS - 1, 2, blocks, rows, LANES), f32), buf, buf],
            tile_flops * 400, "interior",
        )

    def call_project(local):
        return kernel_call(
            lambda *refs: project_edges(local, *refs), send_shapes(1 if local else 0), [], tile_flops * 20, "project"
        )

    partner = lax.ppermute(gradient, "mem", near)
    rim = jnp.concatenate([gradient[:, :TILE], gradient[:, rows - TILE :]], axis=1)
    rim_far = lax.ppermute(rim, "mem", across)
    rim_far_partner = lax.ppermute(rim_far, "mem", near)

    e0, o0, u0 = call_project(True)(perturbations, gradient, partner, counts)
    e0 = lax.ppermute(e0, "strip", even)
    o0 = lax.ppermute(o0, "strip", odd)
    e1, o1, u1 = call_project(False)(perturbations, rim_far, rim_far_partner)
    e1 = lax.ppermute(e1, "strip", even)
    o1 = lax.ppermute(o1, "strip", odd)

    far = lax.ppermute(gradient, "mem", across)
    far_partner = lax.ppermute(far, "mem", near)
    own0, other0 = call_interior(True)(perturbations, gradient, partner, counts)
    own1, other1 = call_interior(False)(perturbations, far, far_partner, counts)
    near0 = lax.ppermute(other0, "mem", near)
    far_sum = own1 + lax.ppermute(other1, "mem", near)
    far1 = lax.ppermute(far_sum, "mem", across)

    eown0, eother0 = call_edges(True)(perturbations, u0, e0, o0, e0, o0, counts)
    eown1, eother1 = call_edges(False)(perturbations, u1, e1, o1, e0, o0, counts)
    enear0 = lax.ppermute(eother0, "mem", near)
    efar_sum = eown1 + lax.ppermute(eother1, "mem", near)
    efar1 = lax.ppermute(efar_sum, "mem", across)

    return kernel_call(
        lambda *refs: finish(scale, *refs), shape(own, rows, ny), [], own * rows * ny * 4, "finish"
    )(own0, near0, far1, eown0, enear0, efar1)


def solution(mesh):
    return jax.shard_map(
        per_device,
        mesh=mesh,
        in_specs=(P("mem", "strip", None), P("mem", None, "strip", None), P("strip", None)),
        out_specs=P("mem", "strip", None),
        check_vma=False,
    )
```

```python
import math

import jax
import jax.numpy as jnp
from jax import lax
from jax.experimental import pallas as pl
from jax.experimental.pallas import tpu as pltpu
from jax.sharding import PartitionSpec as P

SLOTS = 2
VARS = 4
FIELDS = 8
SWEEPS = 4

COEFF_X = 0.35
COEFF_Y = 0.12
CENTRE = 1.0 - 2.0 * COEFF_X - 2.0 * COEFF_Y
RATIO = COEFF_Y / COEFF_X

LANES = 128
TILE = 8
HALF = 16
VMEM_BYTES = 40 * 2**20


def kernel_call(body, out_shape, scratch, flops, name, outside={}):
    def call(*args):
        spaces = [outside.get(i, pltpu.VMEM) for i in range(len(args))]
        return pl.pallas_call(
            body,
            out_shape=out_shape,
            in_specs=[pl.BlockSpec(memory_space=space) for space in spaces],
            out_specs=jax.tree.map(lambda _: pl.BlockSpec(memory_space=pltpu.VMEM), out_shape),
            scratch_shapes=scratch,
            compiler_params=pltpu.CompilerParams(vmem_limit_bytes=VMEM_BYTES),
            cost_estimate=pl.CostEstimate(flops=flops, bytes_accessed=1024, transcendentals=0),
            name=name,
        )(*args)

    return call


def hold(x, *tokens):
    return pl.pallas_call(
        lambda *refs: None,
        out_shape=jax.ShapeDtypeStruct(x.shape, x.dtype),
        in_specs=[pl.BlockSpec(memory_space=pl.ANY)] * (1 + len(tokens)),
        out_specs=pl.BlockSpec(memory_space=pl.ANY),
        input_output_aliases={0: 0},
        cost_estimate=pl.CostEstimate(flops=1, bytes_accessed=1, transcendentals=0),
        name="hold",
    )(x, *tokens)


def lane_masks():
    lane = lax.broadcasted_iota(jnp.int32, (TILE, LANES), 1)
    return lane == 0, lane == LANES - 1


def top_half():
    return lax.broadcasted_iota(jnp.int32, (TILE, LANES), 0) < TILE // 2


def cols(j):
    return pl.ds(j * LANES, LANES)


def sides(values, first, last):
    before = [pltpu.roll(v, 1, 1) for v in values]
    after = [pltpu.roll(v, LANES - 1, 1) for v in values]
    zero = jnp.zeros_like(values[0])
    count = len(values)
    sums = []
    for j in range(count):
        left = jnp.where(first, before[j - 1] if j else zero, before[j])
        right = jnp.where(last, after[j + 1] if j + 1 < count else zero, after[j])
        sums.append(left + right)
    return sums


def order(own):
    shares = VARS // own
    share = lax.axis_index("mem") % shares
    return [at * own + k for at in (share, shares - 1 - share) for k in range(own)]


def fetch(local, own, p_ref, *rest):
    out_ref, sem = rest[-2:]
    members = out_ref.shape[0]
    slot = lax.axis_index("mem") // (VARS // own)
    slot = slot if local else SLOTS - 1 - slot
    copies = [
        pltpu.make_async_copy(p_ref.at[m, pl.ds(slot * VARS, VARS)], out_ref.at[m], sem.at[m]) for m in range(members)
    ]
    for copy in copies:
        copy.start()
    for copy in copies:
        copy.wait()


def weights_of(own, refs):
    return [(ref, k) for ref in refs for k in range(own)]


def project_edges(local, own, p_ref, *rest):
    if local:
        *g_refs, counts_ref, e_ref, o_ref, u_ref = rest
    else:
        *g_refs, _, e_ref, o_ref, u_ref = rest
    members, _, rows, ny = p_ref.shape
    grows = g_refs[0].shape[1]
    even = lax.axis_index("strip") % 2 == 0
    half = top_half()
    fields = order(own)
    grads = weights_of(own, g_refs)

    def put(row, j, top, bottom):
        e_ref[row, :, cols(j)] = jnp.where(even, bottom, top)
        o_ref[row, :, cols(j)] = jnp.where(even, top, bottom)

    if local:
        for j in range(ny // LANES):
            top = counts_ref[0:TILE, cols(j)].astype(jnp.float32)
            bottom = counts_ref[rows - TILE : rows, cols(j)].astype(jnp.float32)
            put(members // 2, j, top, pltpu.roll(bottom, TILE // 2, 0))

    def pair(q, carry):
        for j in range(ny // LANES):
            tops, bottoms = [], []
            for m in (2 * q, 2 * q + 1):
                top = bottom = None
                for f, (g_ref, k) in zip(fields, grads):
                    low = p_ref[m, f, 0:HALF, cols(j)].astype(jnp.float32)[0:TILE]
                    high = p_ref[m, f, rows - HALF : rows, cols(j)].astype(jnp.float32)[HALF - TILE :]
                    low = low * g_ref[k, 0:TILE, cols(j)]
                    high = high * g_ref[k, grows - TILE : grows, cols(j)]
                    top = low if top is None else top + low
                    bottom = high if bottom is None else bottom + high
                u_ref[m, 0:TILE, cols(j)] = top
                u_ref[m, TILE : 2 * TILE, cols(j)] = bottom
                tops.append(top)
                bottoms.append(bottom)
            top = jnp.where(half, tops[0], pltpu.roll(tops[1], TILE // 2, 0))
            bottom = jnp.where(half, pltpu.roll(bottoms[0], TILE // 2, 0), bottoms[1])
            put(q, j, top, bottom)
        return carry

    lax.fori_loop(0, members // 2, pair, 0)


def interior(p_ref, *refs):
    *g_refs, counts_ref, _, own_ref, other_ref, coef, buf_a, buf_b, total_ref = refs
    members, _, rows, ny = p_ref.shape
    own = own_ref.shape[0]
    blocks = ny // LANES
    group = buf_a.shape[0]
    first, last = lane_masks()
    fields = order(own)
    grads = weights_of(own, g_refs)
    sums = [(own_ref, k) for k in range(own)] + [(other_ref, k) for k in range(own)]
    skip = TILE // 2
    whole = list(range(0, rows, TILE))
    kept = list(range(skip, rows - skip, TILE))
    for t in range(1, SWEEPS):
        for j in range(blocks):
            active = (counts_ref[:, cols(j)] > t).astype(jnp.float32)
            total_ref[0, j] = active
            for n, r in enumerate(kept if t == SWEEPS - 1 else whole):
                active = total_ref[0, j, r : r + TILE]
                coef[t - 1, 0, j, n * TILE : (n + 1) * TILE] = active * COEFF_X
                coef[t - 1, 1, j, n * TILE : (n + 1) * TILE] = 1.0 - active * (1.0 - CENTRE)
    zero = jnp.zeros((TILE, LANES), jnp.float32)
    for buf in (buf_a, buf_b):
        for i in range(group):
            for j in range(blocks):
                buf[i, j, 0:TILE] = zero
                buf[i, j, TILE + rows :] = zero
    total_ref[...] = jnp.zeros_like(total_ref)

    def step(s, carry):
        base = s * group
        for r in range(0, rows, HALF):
            for j in range(blocks):
                weights = [g_ref[k, r : r + HALF, cols(j)] for g_ref, k in grads]
                for i in range(group):
                    total = None
                    for f, w in zip(fields, weights):
                        term = p_ref[base + i, f, r : r + HALF, cols(j)].astype(jnp.float32) * w
                        total = term if total is None else total + term
                    buf_a[i, j, TILE + r : TILE + r + HALF] = total
        src, dst = buf_a, buf_b
        for t in range(SWEEPS):
            for n, r in enumerate(kept if t == SWEEPS - 1 else whole):
                at, to = TILE + r, TILE + n * TILE
                for i in range(group):
                    centre = [src[i, j, at : at + TILE] for j in range(blocks)]
                    lateral = sides(centre, first, last)
                    for j in range(blocks):
                        stacked = src[i, j, at - 1 : at - 1 + TILE] + src[i, j, at + 1 : at + 1 + TILE]
                        moved = stacked + RATIO * lateral[j]
                        if t == 0:
                            new = COEFF_X * moved + CENTRE * centre[j]
                        else:
                            own_row = pl.ds(n * TILE, TILE)
                            new = coef[t - 1, 0, j, own_row] * moved + coef[t - 1, 1, j, own_row] * centre[j]
                        dst[i, j, to : to + TILE] = new
            src, dst = dst, src
        for r in range(0, rows, HALF):
            for j in range(blocks):
                smooth = [src[i, j, TILE - skip + r : TILE - skip + r + HALF] for i in range(group)]
                for n, f in enumerate(fields):
                    total = total_ref[n, j, r : r + HALF]
                    for i in range(group):
                        total = total + p_ref[base + i, f, r : r + HALF, cols(j)].astype(jnp.float32) * smooth[i]
                    total_ref[n, j, r : r + HALF] = total
        return carry

    lax.fori_loop(0, members // group, step, 0)
    for n, (ref, k) in enumerate(sums):
        for j in range(blocks):
            for r in range(0, rows - TILE, TILE):
                ref[k, r : r + TILE, cols(j)] = total_ref[n, j, skip + r : skip + r + TILE]


def edges(p_ref, u_ref, e_ref, o_ref, ce_ref, co_ref, counts_ref, _, own_ref, other_ref, coef, buf_a, buf_b, halo):
    members, _, rows, ny = p_ref.shape
    own = own_ref.shape[0]
    blocks = ny // LANES
    first, last = lane_masks()
    half = top_half()
    even = lax.axis_index("strip") % 2 == 0
    fields = order(own)
    sums = [(own_ref, k) for k in range(own)] + [(other_ref, k) for k in range(own)]
    crow = ce_ref.shape[0] - 1
    for j in range(blocks):
        e, o = ce_ref[crow, :, cols(j)], co_ref[crow, :, cols(j)]
        halo[j, 4:12] = jnp.where(even, o, e)
        halo[j, 24:32] = jnp.where(even, e, o)
        halo[j, 8:16] = counts_ref[0:TILE, cols(j)].astype(jnp.float32)
        halo[j, 16:24] = counts_ref[rows - TILE : rows, cols(j)].astype(jnp.float32)

        def weigh(t, to, given):
            active = (given > t).astype(jnp.float32)
            coef[t, 0, j, to : to + TILE] = active * COEFF_X
            coef[t, 1, j, to : to + TILE] = 1.0 - active * (1.0 - CENTRE)

        for to in (8, 16, 24):
            weigh(0, to, halo[j, to - 3 : to + 5])
        for t in range(1, SWEEPS - 1):
            weigh(t, 8, halo[j, 6:14])
            weigh(t, 24, halo[j, 18:26])
        weigh(SWEEPS - 1, 0, jnp.where(half, halo[j, 8:16], halo[j, 16:24]))
    own_ref[...] = jnp.zeros_like(own_ref)
    other_ref[...] = jnp.zeros_like(other_ref)
    plans = [[(5, 8), (13, 16), (21, 24)], [(9, 8), (21, 24)], [(8, 8), (24, 24)]]

    def step(q, carry):
        for j in range(blocks):
            e, o = e_ref[q, :, cols(j)], o_ref[q, :, cols(j)]
            above, below = jnp.where(even, o, e), jnp.where(even, e, o)
            buf_a[0, j, 4:12] = above
            buf_a[0, j, 24:32] = below
            buf_a[1, j, 0:8] = above
            buf_a[1, j, 20:28] = below
            for i in range(2):
                buf_a[i, j, 8:16] = u_ref[2 * q + i, 0:TILE, cols(j)]
                buf_a[i, j, 16:24] = u_ref[2 * q + i, TILE : 2 * TILE, cols(j)]
        src, dst = buf_a, buf_b
        for t in range(SWEEPS - 1):
            for at, to in plans[t]:
                weights = [[coef[t, c, j, to : to + TILE] for j in range(blocks)] for c in range(2)]
                for i in range(2):
                    centre = [src[i, j, at : at + TILE] for j in range(blocks)]
                    lateral = sides(centre, first, last)
                    for j in range(blocks):
                        stacked = src[i, j, at - 1 : at - 1 + TILE] + src[i, j, at + 1 : at + 1 + TILE]
                        moved = stacked + RATIO * lateral[j]
                        dst[i, j, to : to + TILE] = weights[0][j] * moved + weights[1][j] * centre[j]
            src, dst = dst, src

        def both(ref, i, j, shift):
            low, high = ref[i, j, 10 + shift : 18 + shift], ref[i, j, 22 + shift : 30 + shift]
            return jnp.where(half, low, high)

        t = SWEEPS - 1
        weights = [[coef[t, c, j, 0:TILE] for j in range(blocks)] for c in range(2)]
        smooth = []
        for i in range(2):
            centre = [both(src, i, j, 0) for j in range(blocks)]
            lateral = sides(centre, first, last)
            result = []
            for j in range(blocks):
                moved = both(src, i, j, -1) + both(src, i, j, 1) + RATIO * lateral[j]
                result.append(weights[0][j] * moved + weights[1][j] * centre[j])
            smooth.append(result)
        for j in range(blocks):
            for f, (ref, k) in zip(fields, sums):
                total = ref[k, :, cols(j)]
                for i in range(2):
                    low = p_ref[2 * q + i, f, 0:HALF, cols(j)].astype(jnp.float32)[0:TILE]
                    high = p_ref[2 * q + i, f, rows - HALF : rows, cols(j)].astype(jnp.float32)[HALF - TILE :]
                    total = total + jnp.where(half, low, high) * smooth[i][j]
                ref[k, :, cols(j)] = total
        return carry

    lax.fori_loop(0, members // 2, step, 0)


def finish(scale, *refs):
    inner_refs, edge_refs, out_ref = refs[:4], refs[4:8], refs[8]
    own, rows, ny = out_ref.shape
    half = top_half()
    for k in range(own):
        for j in range(ny // LANES):
            edge = sum(ref[k, :, cols(j)] for ref in edge_refs[1:]) + edge_refs[0][k, :, cols(j)]
            parts = [edge]
            for r in range(0, rows - TILE, TILE):
                inner = sum(ref[k, r : r + TILE, cols(j)] for ref in inner_refs[1:]) + inner_refs[0][k, r : r + TILE, cols(j)]
                parts.append(pltpu.roll(inner, TILE // 2, 0))
            parts.append(edge)
            for n in range(rows // TILE):
                out_ref[k, n * TILE : (n + 1) * TILE, cols(j)] = jnp.where(half, parts[n], parts[n + 1]) * scale


def per_device(gradient, perturbations, counts):
    members, _, rows, ny = perturbations.shape
    own = gradient.shape[0]
    mem, strips = lax.axis_size("mem"), lax.axis_size("strip")
    shares = VARS // own
    blocks = ny // LANES
    assert shares == 2 and mem == shares * SLOTS and members % 2 == 0
    scale = 1.0 / math.sqrt(members * mem * FIELDS)
    f32 = jnp.float32

    near = [(i, i ^ 1) for i in range(mem)]
    across = [(i, (i + shares) % mem) for i in range(mem)]
    cross = [(i, (i + shares) % mem ^ 1) for i in range(mem)]
    even = [(i, i ^ 1) for i in range(strips) if i ^ 1 < strips]
    odd = [(i, i + 1) for i in range(1, strips - 1, 2)]
    odd = odd + [(j, i) for i, j in odd]

    def shape(*dims):
        return jax.ShapeDtypeStruct(dims, f32)

    def window(*lead):
        return pltpu.VMEM((*lead, blocks, 40, LANES), f32)

    def call_fetch(local, *token):
        return kernel_call(
            lambda *refs: fetch(local, own, *refs),
            jax.ShapeDtypeStruct((members, VARS, rows, ny), perturbations.dtype),
            [pltpu.SemaphoreType.DMA((members,))], 1024, "fetch", outside={0: pl.ANY, 1: pl.ANY},
        )(pltpu.with_memory_space_constraint(perturbations, pltpu.HBM), *token)

    def call_project(local, *args):
        pairs = members // 2 + (1 if local else 0)
        outs = (shape(pairs, TILE, ny), shape(pairs, TILE, ny), shape(members, 2 * TILE, ny))
        outside = {} if local else {len(args) - 1: pl.ANY}
        body = lambda *refs: project_edges(local, own, *refs)
        return kernel_call(body, outs, [], 1024, "project", outside=outside)(*args)

    def call_interior(*args):
        outs = (shape(own, rows - TILE, ny), shape(own, rows - TILE, ny))
        total = pltpu.VMEM((VARS, blocks, rows, LANES), f32)
        buf = pltpu.VMEM((2, blocks, rows + 2 * TILE, LANES), f32)
        coef = pltpu.VMEM((SWEEPS - 1, 2, blocks, rows, LANES), f32)
        return kernel_call(interior, outs, [coef, buf, buf, total], 1024, "interior", outside={len(args) - 1: pl.ANY})(*args)

    def call_edges(*args):
        outs = (shape(own, TILE, ny), shape(own, TILE, ny))
        scratch = [window(SWEEPS, 2), window(2), window(2), window()]
        return kernel_call(edges, outs, scratch, 1024, "edges", outside={7: pl.ANY})(*args)

    partner = lax.ppermute(gradient, "mem", near)
    far = lax.ppermute(gradient, "mem", across)
    far_partner = lax.ppermute(gradient, "mem", cross)

    p0 = call_fetch(True)
    e0, o0, u0 = call_project(True, p0, gradient, partner, counts)
    e0 = lax.ppermute(e0, "strip", even)
    o0 = lax.ppermute(o0, "strip", odd)
    p1 = call_fetch(False, u0)
    own0, other0 = call_interior(p0, gradient, partner, counts, p1)

    e1, o1, u1 = call_project(False, p1, far, far_partner, own0)
    e1 = lax.ppermute(e1, "strip", even)
    o1 = lax.ppermute(o1, "strip", odd)
    own1, other1 = call_interior(p1, far, far_partner, counts, u1)
    eown0, eother0 = call_edges(p0, u0, e0, o0, e0, o0, counts, own1)
    eown1, eother1 = call_edges(p1, u1, e1, o1, e0, o0, counts, eown0)

    near0 = lax.ppermute(other0, "mem", near)
    far1 = hold(lax.ppermute(own1, "mem", across), near0)
    cross1 = hold(lax.ppermute(other1, "mem", cross), far1)
    enear0 = hold(lax.ppermute(eother0, "mem", near), cross1)
    efar1 = hold(lax.ppermute(eown1, "mem", across), enear0)
    ecross1 = hold(lax.ppermute(eother1, "mem", cross), efar1)

    return kernel_call(
        lambda *refs: finish(scale, *refs), shape(own, rows, ny), [], 1024, "finish"
    )(own0, near0, far1, cross1, eown0, enear0, efar1, ecross1)


def solution(mesh):
    return jax.shard_map(
        per_device,
        mesh=mesh,
        in_specs=(P("mem", "strip", None), P("mem", None, "strip", None), P("strip", None)),
        out_specs=P("mem", "strip", None),
        check_vma=False,
    )
```

```python
import math

import jax
import jax.numpy as jnp
from jax import lax
from jax.experimental import pallas as pl
from jax.experimental.pallas import tpu as pltpu
from jax.sharding import PartitionSpec as P

SLOTS = 2
VARS = 4
FIELDS = 8
SWEEPS = 4

COEFF_X = 0.35
COEFF_Y = 0.12
CENTRE = 1.0 - 2.0 * COEFF_X - 2.0 * COEFF_Y
RATIO = COEFF_Y / COEFF_X

LANES = 128
TILE = 8
HALF = 16
VMEM_BYTES = 40 * 2**20


def kernel_call(body, out_shape, scratch, flops, name, outside={}):
    def call(*args):
        spaces = [outside.get(i, pltpu.VMEM) for i in range(len(args))]
        return pl.pallas_call(
            body,
            out_shape=out_shape,
            in_specs=[pl.BlockSpec(memory_space=space) for space in spaces],
            out_specs=jax.tree.map(lambda _: pl.BlockSpec(memory_space=pltpu.VMEM), out_shape),
            scratch_shapes=scratch,
            compiler_params=pltpu.CompilerParams(vmem_limit_bytes=VMEM_BYTES),
            cost_estimate=pl.CostEstimate(flops=flops, bytes_accessed=1024, transcendentals=0),
            name=name,
        )(*args)

    return call


def lane_masks():
    lane = lax.broadcasted_iota(jnp.int32, (TILE, LANES), 1)
    return lane == 0, lane == LANES - 1


def top_half():
    return lax.broadcasted_iota(jnp.int32, (TILE, LANES), 0) < TILE // 2


def cols(j):
    return pl.ds(j * LANES, LANES)


def sides(values, first, last):
    before = [pltpu.roll(v, 1, 1) for v in values]
    after = [pltpu.roll(v, LANES - 1, 1) for v in values]
    zero = jnp.zeros_like(values[0])
    count = len(values)
    sums = []
    for j in range(count):
        left = jnp.where(first, before[j - 1] if j else zero, before[j])
        right = jnp.where(last, after[j + 1] if j + 1 < count else zero, after[j])
        sums.append(left + right)
    return sums


def order(own):
    shares = VARS // own
    share = lax.axis_index("mem") % shares
    return [at * own + k for at in (share, shares - 1 - share) for k in range(own)]


def fetches(local, own, p_ref, out_ref, sem):
    slot = lax.axis_index("mem") // (VARS // own)
    slot = slot if local else SLOTS - 1 - slot
    return [
        pltpu.make_async_copy(p_ref.at[m, pl.ds(slot * VARS, VARS)], out_ref.at[m], sem.at[m])
        for m in range(out_ref.shape[0])
    ]


def weights_of(own, refs):
    return [(ref, k) for ref in refs for k in range(own)]


def project_edges(local, own, p_ref, *rest):
    if local:
        far_g_ref, far_counts_ref, partner_ref, e_ref, o_ref, u_ref, out_ref, g_ref, counts_ref, sem, small_sem = rest
        copies = fetches(True, own, p_ref, out_ref, sem)
        small = [
            pltpu.make_async_copy(far_g_ref, g_ref, small_sem.at[0]),
            pltpu.make_async_copy(far_counts_ref, counts_ref, small_sem.at[1]),
        ]
        for copy in small + copies:
            copy.start()
        for copy in small:
            copy.wait()
        p_ref, g_refs = out_ref, [g_ref, partner_ref]
    else:
        *g_refs, _, e_ref, o_ref, u_ref = rest
    members, _, rows, ny = p_ref.shape
    grows = g_refs[0].shape[1]
    even = lax.axis_index("strip") % 2 == 0
    half = top_half()
    fields = order(own)
    grads = weights_of(own, g_refs)

    def put(row, j, top, bottom):
        e_ref[row, :, cols(j)] = jnp.where(even, bottom, top)
        o_ref[row, :, cols(j)] = jnp.where(even, top, bottom)

    if local:
        for j in range(ny // LANES):
            top = counts_ref[0:TILE, cols(j)].astype(jnp.float32)
            bottom = counts_ref[rows - TILE : rows, cols(j)].astype(jnp.float32)
            put(members // 2, j, top, pltpu.roll(bottom, TILE // 2, 0))

    def pair(q):
        for j in range(ny // LANES):
            tops, bottoms = [], []
            for m in (2 * q, 2 * q + 1):
                top = bottom = None
                for f, (g_ref, k) in zip(fields, grads):
                    low = p_ref[m, f, 0:HALF, cols(j)].astype(jnp.float32)[0:TILE]
                    high = p_ref[m, f, rows - HALF : rows, cols(j)].astype(jnp.float32)[HALF - TILE :]
                    low = low * g_ref[k, 0:TILE, cols(j)]
                    high = high * g_ref[k, grows - TILE : grows, cols(j)]
                    top = low if top is None else top + low
                    bottom = high if bottom is None else bottom + high
                u_ref[m, 0:TILE, cols(j)] = top
                u_ref[m, TILE : 2 * TILE, cols(j)] = bottom
                tops.append(top)
                bottoms.append(bottom)
            top = jnp.where(half, tops[0], pltpu.roll(tops[1], TILE // 2, 0))
            bottom = jnp.where(half, pltpu.roll(bottoms[0], TILE // 2, 0), bottoms[1])
            put(q, j, top, bottom)

    if local:
        for q in range(members // 2):
            copies[2 * q].wait()
            copies[2 * q + 1].wait()
            pair(q)
    else:
        pl.loop(0, members // 2)(pair)


def interior(local, p_ref, *refs):
    if local:
        *g_refs, counts_ref, rest_ref, own_ref, other_ref, next_ref, coef, buf_a, buf_b, total_ref, sem = refs
        copies = fetches(False, own_ref.shape[0], rest_ref, next_ref, sem)
        for copy in copies:
            copy.start()
    else:
        *g_refs, counts_ref, _, own_ref, other_ref, coef, buf_a, buf_b, total_ref = refs
        copies = []
    members, _, rows, ny = p_ref.shape
    own = own_ref.shape[0]
    blocks = ny // LANES
    group = buf_a.shape[0]
    first, last = lane_masks()
    fields = order(own)
    grads = weights_of(own, g_refs)
    sums = [(own_ref, k) for k in range(own)] + [(other_ref, k) for k in range(own)]
    skip = TILE // 2
    whole = list(range(0, rows, TILE))
    kept = list(range(skip, rows - skip, TILE))
    for t in range(1, SWEEPS):
        for j in range(blocks):
            active = (counts_ref[:, cols(j)] > t).astype(jnp.float32)
            total_ref[0, j] = active
            for n, r in enumerate(kept if t == SWEEPS - 1 else whole):
                active = total_ref[0, j, r : r + TILE]
                coef[t - 1, 0, j, n * TILE : (n + 1) * TILE] = active * COEFF_X
                coef[t - 1, 1, j, n * TILE : (n + 1) * TILE] = 1.0 - active * (1.0 - CENTRE)
    zero = jnp.zeros((TILE, LANES), jnp.float32)
    for buf in (buf_a, buf_b):
        for i in range(group):
            for j in range(blocks):
                buf[i, j, 0:TILE] = zero
                buf[i, j, TILE + rows :] = zero
    total_ref[...] = jnp.zeros_like(total_ref)

    def step(s, carry):
        base = s * group
        for r in range(0, rows, HALF):
            for j in range(blocks):
                weights = [g_ref[k, r : r + HALF, cols(j)] for g_ref, k in grads]
                for i in range(group):
                    total = None
                    for f, w in zip(fields, weights):
                        term = p_ref[base + i, f, r : r + HALF, cols(j)].astype(jnp.float32) * w
                        total = term if total is None else total + term
                    buf_a[i, j, TILE + r : TILE + r + HALF] = total
        src, dst = buf_a, buf_b
        for t in range(SWEEPS):
            for n, r in enumerate(kept if t == SWEEPS - 1 else whole):
                at, to = TILE + r, TILE + n * TILE
                for i in range(group):
                    centre = [src[i, j, at : at + TILE] for j in range(blocks)]
                    lateral = sides(centre, first, last)
                    for j in range(blocks):
                        stacked = src[i, j, at - 1 : at - 1 + TILE] + src[i, j, at + 1 : at + 1 + TILE]
                        moved = stacked + RATIO * lateral[j]
                        if t == 0:
                            new = COEFF_X * moved + CENTRE * centre[j]
                        else:
                            own_row = pl.ds(n * TILE, TILE)
                            new = coef[t - 1, 0, j, own_row] * moved + coef[t - 1, 1, j, own_row] * centre[j]
                        dst[i, j, to : to + TILE] = new
            src, dst = dst, src
        for r in range(0, rows, HALF):
            for j in range(blocks):
                smooth = [src[i, j, TILE - skip + r : TILE - skip + r + HALF] for i in range(group)]
                for n, f in enumerate(fields):
                    total = total_ref[n, j, r : r + HALF]
                    for i in range(group):
                        total = total + p_ref[base + i, f, r : r + HALF, cols(j)].astype(jnp.float32) * smooth[i]
                    total_ref[n, j, r : r + HALF] = total
        return carry

    lax.fori_loop(0, members // group, step, 0)
    for n, (ref, k) in enumerate(sums):
        for j in range(blocks):
            for r in range(0, rows - TILE, TILE):
                ref[k, r : r + TILE, cols(j)] = total_ref[n, j, skip + r : skip + r + TILE]
    for copy in copies:
        copy.wait()


def edges(p_ref, u_ref, e_ref, o_ref, ce_ref, co_ref, counts_ref, _, own_ref, other_ref, coef, buf_a, buf_b, halo):
    members, _, rows, ny = p_ref.shape
    own = own_ref.shape[0]
    blocks = ny // LANES
    first, last = lane_masks()
    half = top_half()
    even = lax.axis_index("strip") % 2 == 0
    fields = order(own)
    sums = [(own_ref, k) for k in range(own)] + [(other_ref, k) for k in range(own)]
    crow = ce_ref.shape[0] - 1
    for j in range(blocks):
        e, o = ce_ref[crow, :, cols(j)], co_ref[crow, :, cols(j)]
        halo[j, 4:12] = jnp.where(even, o, e)
        halo[j, 24:32] = jnp.where(even, e, o)
        halo[j, 8:16] = counts_ref[0:TILE, cols(j)].astype(jnp.float32)
        halo[j, 16:24] = counts_ref[rows - TILE : rows, cols(j)].astype(jnp.float32)

        def weigh(t, to, given):
            active = (given > t).astype(jnp.float32)
            coef[t, 0, j, to : to + TILE] = active * COEFF_X
            coef[t, 1, j, to : to + TILE] = 1.0 - active * (1.0 - CENTRE)

        for to in (8, 16, 24):
            weigh(0, to, halo[j, to - 3 : to + 5])
        for t in range(1, SWEEPS - 1):
            weigh(t, 8, halo[j, 6:14])
            weigh(t, 24, halo[j, 18:26])
        weigh(SWEEPS - 1, 0, jnp.where(half, halo[j, 8:16], halo[j, 16:24]))
    own_ref[...] = jnp.zeros_like(own_ref)
    other_ref[...] = jnp.zeros_like(other_ref)
    plans = [[(5, 8), (13, 16), (21, 24)], [(9, 8), (21, 24)], [(8, 8), (24, 24)]]

    def step(q, carry):
        for j in range(blocks):
            e, o = e_ref[q, :, cols(j)], o_ref[q, :, cols(j)]
            above, below = jnp.where(even, o, e), jnp.where(even, e, o)
            buf_a[0, j, 4:12] = above
            buf_a[0, j, 24:32] = below
            buf_a[1, j, 0:8] = above
            buf_a[1, j, 20:28] = below
            for i in range(2):
                buf_a[i, j, 8:16] = u_ref[2 * q + i, 0:TILE, cols(j)]
                buf_a[i, j, 16:24] = u_ref[2 * q + i, TILE : 2 * TILE, cols(j)]
        src, dst = buf_a, buf_b
        for t in range(SWEEPS - 1):
            for at, to in plans[t]:
                weights = [[coef[t, c, j, to : to + TILE] for j in range(blocks)] for c in range(2)]
                for i in range(2):
                    centre = [src[i, j, at : at + TILE] for j in range(blocks)]
                    lateral = sides(centre, first, last)
                    for j in range(blocks):
                        stacked = src[i, j, at - 1 : at - 1 + TILE] + src[i, j, at + 1 : at + 1 + TILE]
                        moved = stacked + RATIO * lateral[j]
                        dst[i, j, to : to + TILE] = weights[0][j] * moved + weights[1][j] * centre[j]
            src, dst = dst, src

        def both(ref, i, j, shift):
            low, high = ref[i, j, 10 + shift : 18 + shift], ref[i, j, 22 + shift : 30 + shift]
            return jnp.where(half, low, high)

        t = SWEEPS - 1
        weights = [[coef[t, c, j, 0:TILE] for j in range(blocks)] for c in range(2)]
        smooth = []
        for i in range(2):
            centre = [both(src, i, j, 0) for j in range(blocks)]
            lateral = sides(centre, first, last)
            result = []
            for j in range(blocks):
                moved = both(src, i, j, -1) + both(src, i, j, 1) + RATIO * lateral[j]
                result.append(weights[0][j] * moved + weights[1][j] * centre[j])
            smooth.append(result)
        for j in range(blocks):
            for f, (ref, k) in zip(fields, sums):
                total = ref[k, :, cols(j)]
                for i in range(2):
                    low = p_ref[2 * q + i, f, 0:HALF, cols(j)].astype(jnp.float32)[0:TILE]
                    high = p_ref[2 * q + i, f, rows - HALF : rows, cols(j)].astype(jnp.float32)[HALF - TILE :]
                    total = total + jnp.where(half, low, high) * smooth[i][j]
                ref[k, :, cols(j)] = total
        return carry

    lax.fori_loop(0, members // 2, step, 0)


def finish(scale, *refs):
    inner_ref, *edge_refs, out_ref = refs
    own, rows, ny = out_ref.shape
    half = top_half()
    for k in range(own):
        for j in range(ny // LANES):
            edge = sum(ref[k, :, cols(j)] for ref in edge_refs[1:]) + edge_refs[0][k, :, cols(j)]
            parts = [edge]
            for r in range(0, rows - TILE, TILE):
                parts.append(pltpu.roll(inner_ref[k, r : r + TILE, cols(j)], TILE // 2, 0))
            parts.append(edge)
            for n in range(rows // TILE):
                out_ref[k, n * TILE : (n + 1) * TILE, cols(j)] = jnp.where(half, parts[n], parts[n + 1]) * scale


def per_device(gradient, perturbations, counts):
    members, _, rows, ny = perturbations.shape
    own = gradient.shape[0]
    mem, strips = lax.axis_size("mem"), lax.axis_size("strip")
    shares = VARS // own
    blocks = ny // LANES
    assert shares == 2 and mem == shares * SLOTS and members % 2 == 0
    scale = 1.0 / math.sqrt(members * mem * FIELDS)
    f32 = jnp.float32

    near = [(i, i ^ 1) for i in range(mem)]
    across = [(i, (i + shares) % mem) for i in range(mem)]
    cross = [(i, (i + shares) % mem ^ 1) for i in range(mem)]
    even = [(i, i ^ 1) for i in range(strips) if i ^ 1 < strips]
    odd = [(i, i + 1) for i in range(1, strips - 1, 2)]
    odd = odd + [(j, i) for i, j in odd]

    def shape(*dims):
        return jax.ShapeDtypeStruct(dims, f32)

    def window(*lead):
        return pltpu.VMEM((*lead, blocks, 40, LANES), f32)

    stored, stored_g, stored_counts = (
        pltpu.with_memory_space_constraint(x, pltpu.HBM) for x in (perturbations, gradient, counts)
    )
    one_slot = jax.ShapeDtypeStruct((members, VARS, rows, ny), perturbations.dtype)
    copy_sem = pltpu.SemaphoreType.DMA((members,))

    def call_project(local, *args):
        pairs = members // 2 + (1 if local else 0)
        outs = (shape(pairs, TILE, ny), shape(pairs, TILE, ny), shape(members, 2 * TILE, ny))
        outs = outs + ((one_slot, shape(own, rows, ny), jax.ShapeDtypeStruct((rows, ny), counts.dtype)) if local else ())
        outside = {0: pl.ANY, 1: pl.ANY, 2: pl.ANY} if local else {len(args) - 1: pl.ANY}
        body = lambda *refs: project_edges(local, own, *refs)
        return kernel_call(body, outs, [copy_sem, pltpu.SemaphoreType.DMA((2,))] if local else [], 1024, "project", outside=outside)(*args)

    def call_interior(local, *args):
        outs = (shape(own, rows - TILE, ny), shape(own, rows - TILE, ny)) + ((one_slot,) if local else ())
        total = pltpu.VMEM((VARS, blocks, rows, LANES), f32)
        buf = pltpu.VMEM((2, blocks, rows + 2 * TILE, LANES), f32)
        coef = pltpu.VMEM((SWEEPS - 1, 2, blocks, rows, LANES), f32)
        scratch = [coef, buf, buf, total] + ([copy_sem] if local else [])
        body = lambda *refs: interior(local, *refs)
        return kernel_call(body, outs, scratch, 1024, "interior", outside={len(args) - 1: pl.ANY})(*args)

    def call_edges(*args):
        outs = (shape(own, TILE, ny), shape(own, TILE, ny))
        scratch = [window(SWEEPS, 2), window(2), window(2), window()]
        return kernel_call(edges, outs, scratch, 1024, "edges", outside={7: pl.ANY})(*args)

    partner = lax.ppermute(gradient, "mem", near)
    far = lax.ppermute(gradient, "mem", across)
    far_partner = lax.ppermute(gradient, "mem", cross)

    e0, o0, u0, p0, near_g, near_counts = call_project(True, stored, stored_g, stored_counts, partner)
    e0 = lax.ppermute(e0, "strip", even)
    o0 = lax.ppermute(o0, "strip", odd)
    own0, other0, p1 = call_interior(True, p0, near_g, partner, near_counts, stored)

    e1, o1, u1 = call_project(False, p1, far, far_partner, own0)
    e1 = lax.ppermute(e1, "strip", even)
    o1 = lax.ppermute(o1, "strip", odd)
    own1, other1 = call_interior(False, p1, far, far_partner, near_counts, u1)
    eown0, eother0 = call_edges(p0, u0, e0, o0, e0, o0, near_counts, own1)
    eown1, eother1 = call_edges(p1, u1, e1, o1, e0, o0, near_counts, eown0)

    inner = own0 + lax.ppermute(other0, "mem", near)
    inner = inner + lax.ppermute(own1, "mem", across)
    inner = inner + lax.ppermute(other1, "mem", cross)
    enear0 = lax.ppermute(eother0, "mem", near)
    efar1 = lax.ppermute(eown1, "mem", across)
    ecross1 = lax.ppermute(eother1, "mem", cross)
    return kernel_call(
        lambda *refs: finish(scale, *refs), shape(own, rows, ny), [], 1024, "finish"
    )(inner, eown0, enear0, efar1, ecross1)


def solution(mesh):
    return jax.shard_map(
        per_device,
        mesh=mesh,
        in_specs=(P("mem", "strip", None), P("mem", None, "strip", None), P("strip", None)),
        out_specs=P("mem", "strip", None),
        check_vma=False,
    )
```

```python
import math

import jax
import jax.numpy as jnp
from jax import lax
from jax.experimental import pallas as pl
from jax.experimental.pallas import tpu as pltpu
from jax.sharding import PartitionSpec as P

SLOTS = 2
VARS = 4
FIELDS = 8
SWEEPS = 4

COEFF_X = 0.35
COEFF_Y = 0.12
CENTRE = 1.0 - 2.0 * COEFF_X - 2.0 * COEFF_Y
RATIO = COEFF_Y / COEFF_X

LANES = 128
TILE = 8
HALF = 16
VMEM_BYTES = 40 * 2**20


def kernel_call(body, out_shape, scratch, flops, name, outside={}):
    def call(*args):
        spaces = [outside.get(i, pltpu.VMEM) for i in range(len(args))]
        return pl.pallas_call(
            body,
            out_shape=out_shape,
            in_specs=[pl.BlockSpec(memory_space=space) for space in spaces],
            out_specs=jax.tree.map(lambda _: pl.BlockSpec(memory_space=pltpu.VMEM), out_shape),
            scratch_shapes=scratch,
            compiler_params=pltpu.CompilerParams(vmem_limit_bytes=VMEM_BYTES),
            cost_estimate=pl.CostEstimate(flops=flops, bytes_accessed=1024, transcendentals=0),
            name=name,
        )(*args)

    return call


def lane_masks():
    lane = lax.broadcasted_iota(jnp.int32, (TILE, LANES), 1)
    return lane == 0, lane == LANES - 1


def top_half():
    return lax.broadcasted_iota(jnp.int32, (TILE, LANES), 0) < TILE // 2


def cols(j):
    return pl.ds(j * LANES, LANES)


def sides(values, first, last):
    before = [pltpu.roll(v, 1, 1) for v in values]
    after = [pltpu.roll(v, LANES - 1, 1) for v in values]
    zero = jnp.zeros_like(values[0])
    count = len(values)
    sums = []
    for j in range(count):
        left = jnp.where(first, before[j - 1] if j else zero, before[j])
        right = jnp.where(last, after[j + 1] if j + 1 < count else zero, after[j])
        sums.append(left + right)
    return sums


def order(own):
    shares = VARS // own
    share = lax.axis_index("mem") % shares
    return [at * own + k for at in (share, shares - 1 - share) for k in range(own)]


def fetches(local, own, p_ref, out_ref, sem):
    slot = lax.axis_index("mem") // (VARS // own)
    slot = slot if local else SLOTS - 1 - slot
    return [
        pltpu.make_async_copy(p_ref.at[m, pl.ds(slot * VARS, VARS)], out_ref.at[m], sem.at[m])
        for m in range(out_ref.shape[0])
    ]


def weights_of(own, refs):
    return [(ref, k) for ref in refs for k in range(own)]


def project_edges(local, own, p_ref, *rest):
    if local:
        far_g_ref, far_counts_ref, partner_ref, e_ref, o_ref, out_ref, g_ref, counts_ref, sem, small_sem = rest
        copies = fetches(True, own, p_ref, out_ref, sem)
        small = [
            pltpu.make_async_copy(far_g_ref, g_ref, small_sem.at[0]),
            pltpu.make_async_copy(far_counts_ref, counts_ref, small_sem.at[1]),
        ]
        for copy in small + copies:
            copy.start()
        for copy in small:
            copy.wait()
        p_ref, g_refs = out_ref, [g_ref, partner_ref]
    else:
        *g_refs, e_ref, o_ref, u_ref = rest
    members, _, rows, ny = p_ref.shape
    even = lax.axis_index("strip") % 2 == 0
    half = top_half()
    fields = order(own)
    grads = weights_of(own, g_refs)

    def put(row, j, top, bottom):
        e_ref[row, :, cols(j)] = jnp.where(even, bottom, top)
        o_ref[row, :, cols(j)] = jnp.where(even, top, bottom)

    if local:
        for j in range(ny // LANES):
            top = counts_ref[0:TILE, cols(j)].astype(jnp.float32)
            bottom = counts_ref[rows - TILE : rows, cols(j)].astype(jnp.float32)
            put(members // 2, j, top, pltpu.roll(bottom, TILE // 2, 0))

    def pair(q):
        for j in range(ny // LANES):
            tops, bottoms = [], []
            for m in (2 * q, 2 * q + 1):
                top = bottom = None
                for f, (g_ref, k) in zip(fields, grads):
                    low = p_ref[m, f, 0:HALF, cols(j)].astype(jnp.float32)[0:TILE]
                    high = p_ref[m, f, rows - HALF : rows, cols(j)].astype(jnp.float32)[HALF - TILE :]
                    low = low * g_ref[k, 0:TILE, cols(j)]
                    high = high * g_ref[k, g_ref.shape[1] - TILE : g_ref.shape[1], cols(j)]
                    top = low if top is None else top + low
                    bottom = high if bottom is None else bottom + high
                if not local:
                    u_ref[m, 0:TILE, cols(j)] = top
                    u_ref[m, TILE : 2 * TILE, cols(j)] = bottom
                tops.append(top)
                bottoms.append(bottom)
            top = jnp.where(half, tops[0], pltpu.roll(tops[1], TILE // 2, 0))
            bottom = jnp.where(half, pltpu.roll(bottoms[0], TILE // 2, 0), bottoms[1])
            put(q, j, top, bottom)

    if local:
        for q in range(members // 2):
            copies[2 * q].wait()
            copies[2 * q + 1].wait()
            pair(q)
    else:
        pl.loop(0, members // 2)(pair)


def interior(p_ref, ga_ref, gb_ref, counts_ref, _, own_ref, other_ref, coef, buf_a, buf_b, total_ref):
    g_refs = ga_ref, gb_ref
    members, _, rows, ny = p_ref.shape
    own = own_ref.shape[0]
    blocks = ny // LANES
    group = buf_a.shape[0]
    first, last = lane_masks()
    fields = order(own)
    grads = weights_of(own, g_refs)
    sums = [(own_ref, k) for k in range(own)] + [(other_ref, k) for k in range(own)]
    skip = TILE // 2
    whole = list(range(0, rows, TILE))
    kept = list(range(skip, rows - skip, TILE))
    for t in range(1, SWEEPS):
        for j in range(blocks):
            active = (counts_ref[:, cols(j)] > t).astype(jnp.float32)
            total_ref[0, j] = active
            for n, r in enumerate(kept if t == SWEEPS - 1 else whole):
                active = total_ref[0, j, r : r + TILE]
                coef[t - 1, 0, j, n * TILE : (n + 1) * TILE] = active * COEFF_X
                coef[t - 1, 1, j, n * TILE : (n + 1) * TILE] = 1.0 - active * (1.0 - CENTRE)
    zero = jnp.zeros((TILE, LANES), jnp.float32)
    for buf in (buf_a, buf_b):
        for i in range(group):
            for j in range(blocks):
                buf[i, j, 0:TILE] = zero
                buf[i, j, TILE + rows :] = zero
    total_ref[...] = jnp.zeros_like(total_ref)

    def step(s, carry):
        base = s * group
        for r in range(0, rows, HALF):
            for j in range(blocks):
                weights = [g_ref[k, r : r + HALF, cols(j)] for g_ref, k in grads]
                for i in range(group):
                    total = None
                    for f, w in zip(fields, weights):
                        term = p_ref[base + i, f, r : r + HALF, cols(j)].astype(jnp.float32) * w
                        total = term if total is None else total + term
                    buf_a[i, j, TILE + r : TILE + r + HALF] = total
        src, dst = buf_a, buf_b
        for t in range(SWEEPS):
            for n, r in enumerate(kept if t == SWEEPS - 1 else whole):
                at, to = TILE + r, TILE + n * TILE
                for i in range(group):
                    centre = [src[i, j, at : at + TILE] for j in range(blocks)]
                    lateral = sides(centre, first, last)
                    for j in range(blocks):
                        stacked = src[i, j, at - 1 : at - 1 + TILE] + src[i, j, at + 1 : at + 1 + TILE]
                        moved = stacked + RATIO * lateral[j]
                        if t == 0:
                            new = COEFF_X * moved + CENTRE * centre[j]
                        else:
                            own_row = pl.ds(n * TILE, TILE)
                            new = coef[t - 1, 0, j, own_row] * moved + coef[t - 1, 1, j, own_row] * centre[j]
                        dst[i, j, to : to + TILE] = new
            src, dst = dst, src
        for r in range(0, rows, HALF):
            for j in range(blocks):
                smooth = [src[i, j, TILE - skip + r : TILE - skip + r + HALF] for i in range(group)]
                for n, f in enumerate(fields):
                    total = total_ref[n, j, r : r + HALF]
                    for i in range(group):
                        total = total + p_ref[base + i, f, r : r + HALF, cols(j)].astype(jnp.float32) * smooth[i]
                    total_ref[n, j, r : r + HALF] = total
        return carry

    lax.fori_loop(0, members // group, step, 0)
    for n, (ref, k) in enumerate(sums):
        for j in range(blocks):
            for r in range(0, rows - TILE, TILE):
                ref[k, r : r + TILE, cols(j)] = total_ref[n, j, skip + r : skip + r + TILE]


def fetch(own, p_ref, _, out_ref, sem):
    copies = fetches(False, own, p_ref, out_ref, sem)
    for copy in copies:
        copy.start()
    for copy in copies:
        copy.wait()


def relay(*refs):
    count = len(refs) // 2
    for ref, out_ref in zip(refs[:count], refs[count + 1 :]):
        out_ref[...] = ref[...]


def whole(p_ref, ga_ref, gb_ref, e_ref, o_ref, counts_ref, _, own_ref, other_ref, coef, buf_a, buf_b):
    members, _, rows, ny = p_ref.shape
    own = own_ref.shape[0]
    blocks = ny // LANES
    first, last = lane_masks()
    even = lax.axis_index("strip") % 2 == 0
    fields = order(own)
    grads = weights_of(own, (ga_ref, gb_ref))
    sums = [(own_ref, k) for k in range(own)] + [(other_ref, k) for k in range(own)]
    count = [-(-(rows + 2 * (SWEEPS - 1 - t)) // TILE) for t in range(SWEEPS)]
    start = TILE + TILE // 2

    def place(dst, j, at_odd, e, o):
        above, below = jnp.where(even, o, e), jnp.where(even, e, o)
        if at_odd:
            dst[j, TILE : 2 * TILE] = above
            dst[j, start + rows : start + rows + TILE] = below
        else:
            dst[j, start : start + TILE] = above
            dst[j, 2 * TILE + rows : 3 * TILE + rows] = below

    for j in range(blocks):
        counted = buf_b.at[0]
        place(counted, j, False, e_ref[members // 2, :, cols(j)], o_ref[members // 2, :, cols(j)])
        counted[j, 2 * TILE : 2 * TILE + rows] = counts_ref[:, cols(j)].astype(jnp.float32)
        for t in range(SWEEPS):
            for n in range(count[t]):
                at = start + 1 + t + n * TILE
                active = (counted[j, at : at + TILE] > t).astype(jnp.float32)
                coef[t, 0, j, n * TILE : (n + 1) * TILE] = active * COEFF_X
                coef[t, 1, j, n * TILE : (n + 1) * TILE] = 1.0 - active * (1.0 - CENTRE)
    own_ref[...] = jnp.zeros_like(own_ref)
    other_ref[...] = jnp.zeros_like(other_ref)

    def step(q, carry):
        for j in range(blocks):
            for i in range(2):
                place(buf_a.at[i], j, i == 1, e_ref[q, :, cols(j)], o_ref[q, :, cols(j)])
        for r in range(0, rows, HALF):
            for j in range(blocks):
                weights = [g_ref[k, r : r + HALF, cols(j)] for g_ref, k in grads]
                for i in range(2):
                    total = None
                    for f, w in zip(fields, weights):
                        term = p_ref[2 * q + i, f, r : r + HALF, cols(j)].astype(jnp.float32) * w
                        total = term if total is None else total + term
                    buf_a[i, j, 2 * TILE + r : 2 * TILE + r + HALF] = total
        src, dst = buf_a, buf_b
        for t in range(SWEEPS):
            for n in range(count[t]):
                at, to = (TILE if t else start) + 1 + n * TILE, TILE + n * TILE
                weights = [[coef[t, c, j, n * TILE : (n + 1) * TILE] for j in range(blocks)] for c in range(2)]
                for i in range(2):
                    centre = [src[i, j, at : at + TILE] for j in range(blocks)]
                    lateral = sides(centre, first, last)
                    for j in range(blocks):
                        stacked = src[i, j, at - 1 : at - 1 + TILE] + src[i, j, at + 1 : at + 1 + TILE]
                        moved = stacked + RATIO * lateral[j]
                        dst[i, j, to : to + TILE] = weights[0][j] * moved + weights[1][j] * centre[j]
            src, dst = dst, src
        for r in range(0, rows, HALF):
            for j in range(blocks):
                smooth = [src[i, j, TILE + r : TILE + r + HALF] for i in range(2)]
                for f, (ref, k) in zip(fields, sums):
                    total = ref[k, r : r + HALF, cols(j)]
                    for i in range(2):
                        total = total + p_ref[2 * q + i, f, r : r + HALF, cols(j)].astype(jnp.float32) * smooth[i]
                    ref[k, r : r + HALF, cols(j)] = total
        return carry

    lax.fori_loop(0, members // 2, step, 0)


def edges(p_ref, u_ref, e_ref, o_ref, ce_ref, co_ref, counts_ref, _, own_ref, other_ref, coef, buf_a, buf_b, halo):
    members, _, rows, ny = p_ref.shape
    own = own_ref.shape[0]
    blocks = ny // LANES
    first, last = lane_masks()
    half = top_half()
    even = lax.axis_index("strip") % 2 == 0
    fields = order(own)
    sums = [(own_ref, k) for k in range(own)] + [(other_ref, k) for k in range(own)]
    crow = ce_ref.shape[0] - 1
    for j in range(blocks):
        e, o = ce_ref[crow, :, cols(j)], co_ref[crow, :, cols(j)]
        halo[j, 4:12] = jnp.where(even, o, e)
        halo[j, 24:32] = jnp.where(even, e, o)
        halo[j, 8:16] = counts_ref[0:TILE, cols(j)].astype(jnp.float32)
        halo[j, 16:24] = counts_ref[rows - TILE : rows, cols(j)].astype(jnp.float32)

        def weigh(t, to, given):
            active = (given > t).astype(jnp.float32)
            coef[t, 0, j, to : to + TILE] = active * COEFF_X
            coef[t, 1, j, to : to + TILE] = 1.0 - active * (1.0 - CENTRE)

        for to in (8, 16, 24):
            weigh(0, to, halo[j, to - 3 : to + 5])
        for t in range(1, SWEEPS - 1):
            weigh(t, 8, halo[j, 6:14])
            weigh(t, 24, halo[j, 18:26])
        weigh(SWEEPS - 1, 0, jnp.where(half, halo[j, 8:16], halo[j, 16:24]))
    own_ref[...] = jnp.zeros_like(own_ref)
    other_ref[...] = jnp.zeros_like(other_ref)
    plans = [[(5, 8), (13, 16), (21, 24)], [(9, 8), (21, 24)], [(8, 8), (24, 24)]]

    def step(q, carry):
        for j in range(blocks):
            e, o = e_ref[q, :, cols(j)], o_ref[q, :, cols(j)]
            above, below = jnp.where(even, o, e), jnp.where(even, e, o)
            buf_a[0, j, 4:12] = above
            buf_a[0, j, 24:32] = below
            buf_a[1, j, 0:8] = above
            buf_a[1, j, 20:28] = below
            for i in range(2):
                buf_a[i, j, 8:16] = u_ref[2 * q + i, 0:TILE, cols(j)]
                buf_a[i, j, 16:24] = u_ref[2 * q + i, TILE : 2 * TILE, cols(j)]
        src, dst = buf_a, buf_b
        for t in range(SWEEPS - 1):
            for at, to in plans[t]:
                weights = [[coef[t, c, j, to : to + TILE] for j in range(blocks)] for c in range(2)]
                for i in range(2):
                    centre = [src[i, j, at : at + TILE] for j in range(blocks)]
                    lateral = sides(centre, first, last)
                    for j in range(blocks):
                        stacked = src[i, j, at - 1 : at - 1 + TILE] + src[i, j, at + 1 : at + 1 + TILE]
                        moved = stacked + RATIO * lateral[j]
                        dst[i, j, to : to + TILE] = weights[0][j] * moved + weights[1][j] * centre[j]
            src, dst = dst, src

        def both(ref, i, j, shift):
            low, high = ref[i, j, 10 + shift : 18 + shift], ref[i, j, 22 + shift : 30 + shift]
            return jnp.where(half, low, high)

        t = SWEEPS - 1
        weights = [[coef[t, c, j, 0:TILE] for j in range(blocks)] for c in range(2)]
        smooth = []
        for i in range(2):
            centre = [both(src, i, j, 0) for j in range(blocks)]
            lateral = sides(centre, first, last)
            result = []
            for j in range(blocks):
                moved = both(src, i, j, -1) + both(src, i, j, 1) + RATIO * lateral[j]
                result.append(weights[0][j] * moved + weights[1][j] * centre[j])
            smooth.append(result)
        for j in range(blocks):
            for f, (ref, k) in zip(fields, sums):
                total = ref[k, :, cols(j)]
                for i in range(2):
                    low = p_ref[2 * q + i, f, 0:HALF, cols(j)].astype(jnp.float32)[0:TILE]
                    high = p_ref[2 * q + i, f, rows - HALF : rows, cols(j)].astype(jnp.float32)[HALF - TILE :]
                    total = total + jnp.where(half, low, high) * smooth[i][j]
                ref[k, :, cols(j)] = total
        return carry

    lax.fori_loop(0, members // 2, step, 0)


def finish(scale, own_ref, near_ref, inner_ref, *refs):
    *edge_refs, out_ref = refs
    own, rows, ny = out_ref.shape
    half = top_half()
    for k in range(own):
        for j in range(ny // LANES):
            edge = edge_refs[0][k, :, cols(j)] + edge_refs[1][k, :, cols(j)]
            parts = [edge]
            for r in range(0, rows - TILE, TILE):
                parts.append(pltpu.roll(inner_ref[k, r : r + TILE, cols(j)], TILE // 2, 0))
            parts.append(edge)
            for n in range(rows // TILE):
                far = jnp.where(half, parts[n], parts[n + 1])
                tile = pl.ds(n * TILE, TILE)
                out_ref[k, tile, cols(j)] = (own_ref[k, tile, cols(j)] + near_ref[k, tile, cols(j)] + far) * scale


def per_device(gradient, perturbations, counts):
    members, _, rows, ny = perturbations.shape
    own = gradient.shape[0]
    mem, strips = lax.axis_size("mem"), lax.axis_size("strip")
    shares = VARS // own
    blocks = ny // LANES
    assert shares == 2 and mem == shares * SLOTS and members % 2 == 0
    scale = 1.0 / math.sqrt(members * mem * FIELDS)
    f32 = jnp.float32

    near = [(i, i ^ 1) for i in range(mem)]
    across = [(i, (i + shares) % mem) for i in range(mem)]
    cross = [(i, (i + shares) % mem ^ 1) for i in range(mem)]
    even = [(i, i ^ 1) for i in range(strips) if i ^ 1 < strips]
    odd = [(i, i + 1) for i in range(1, strips - 1, 2)]
    odd = odd + [(j, i) for i, j in odd]

    def shape(*dims):
        return jax.ShapeDtypeStruct(dims, f32)

    def window(*lead):
        return pltpu.VMEM((*lead, blocks, 40, LANES), f32)

    stored, stored_g, stored_counts = (
        pltpu.with_memory_space_constraint(x, pltpu.HBM) for x in (perturbations, gradient, counts)
    )
    one_slot = jax.ShapeDtypeStruct((members, VARS, rows, ny), perturbations.dtype)
    copy_sem = pltpu.SemaphoreType.DMA((members,))

    def call_project(local, *args):
        pairs = members // 2 + (1 if local else 0)
        outs = (shape(pairs, TILE, ny), shape(pairs, TILE, ny))
        if local:
            outs = outs + (one_slot, shape(own, rows, ny), jax.ShapeDtypeStruct((rows, ny), counts.dtype))
        else:
            outs = outs + (shape(members, 2 * TILE, ny),)
        outside = {0: pl.ANY, 1: pl.ANY, 2: pl.ANY} if local else {}
        scratch = [copy_sem, pltpu.SemaphoreType.DMA((2,))] if local else []
        body = lambda *refs: project_edges(local, own, *refs)
        return kernel_call(body, outs, scratch, 1024, "project", outside=outside)(*args)

    def call_fetch(*args):
        body = lambda *refs: fetch(own, *refs)
        return kernel_call(body, one_slot, [copy_sem], 1024, "fetch", outside={0: pl.ANY, 1: pl.ANY})(*args)

    def call_relay(*args):
        outs = tuple(shape(*x.shape) for x in args[:-1])
        return kernel_call(relay, outs, [], 1024, "relay", outside={len(outs): pl.ANY})(*args)

    def call_interior(*args):
        outs = (shape(own, rows - TILE, ny), shape(own, rows - TILE, ny))
        total = pltpu.VMEM((VARS, blocks, rows, LANES), f32)
        buf = pltpu.VMEM((2, blocks, rows + 2 * TILE, LANES), f32)
        coef = pltpu.VMEM((SWEEPS - 1, 2, blocks, rows, LANES), f32)
        return kernel_call(interior, outs, [coef, buf, buf, total], 1024, "interior", outside={4: pl.ANY})(*args)

    def call_whole(*args):
        outs = (shape(own, rows, ny), shape(own, rows, ny))
        buf = pltpu.VMEM((2, blocks, rows + 3 * TILE, LANES), f32)
        coef = pltpu.VMEM((SWEEPS, 2, blocks, rows + TILE, LANES), f32)
        return kernel_call(whole, outs, [coef, buf, buf], 1024, "whole", outside={6: pl.ANY})(*args)

    def call_edges(*args):
        outs = (shape(own, TILE, ny), shape(own, TILE, ny))
        scratch = [window(SWEEPS, 2), window(2), window(2), window()]
        return kernel_call(edges, outs, scratch, 1024, "edges", outside={7: pl.ANY})(*args)

    partner = lax.ppermute(gradient, "mem", near)
    rim = jnp.concatenate([gradient[:, :TILE], gradient[:, rows - TILE :]], axis=1)
    far_rim = lax.ppermute(rim, "mem", cross)
    far = lax.ppermute(gradient, "mem", across)
    e0, o0, p0, near_g, near_counts = call_project(True, stored, stored_g, stored_counts, partner)
    e0 = lax.ppermute(e0, "strip", even)
    o0 = lax.ppermute(o0, "strip", odd)
    p1 = call_fetch(stored, near_counts)
    e1, o1, u1 = call_project(False, p1, far, far_rim)
    far_partner = lax.ppermute(call_relay(far, u1)[0], "mem", near)
    e1 = lax.ppermute(e1, "strip", even)
    o1 = lax.ppermute(o1, "strip", odd)
    own1, other1 = call_interior(p1, far, far_partner, near_counts, u1)
    own0, other0 = call_whole(p0, near_g, partner, e0, o0, near_counts, own1)
    eown1, eother1 = call_edges(p1, u1, e1, o1, e0, o0, near_counts, own0)

    near0 = lax.ppermute(other0, "mem", near)
    inner = lax.ppermute(own1, "mem", across) + lax.ppermute(other1, "mem", cross)
    eown1, eother1 = call_relay(eown1, eother1, inner)
    efar1 = lax.ppermute(eown1, "mem", across)
    ecross1 = lax.ppermute(eother1, "mem", cross)
    return kernel_call(
        lambda *refs: finish(scale, *refs), shape(own, rows, ny), [], 1024, "finish"
    )(own0, near0, inner, efar1, ecross1)


def solution(mesh):
    return jax.shard_map(
        per_device,
        mesh=mesh,
        in_specs=(P("mem", "strip", None), P("mem", None, "strip", None), P("strip", None)),
        out_specs=P("mem", "strip", None),
        check_vma=False,
    )
```

```python
import math

import jax
import jax.numpy as jnp
from jax import lax
from jax.experimental import pallas as pl
from jax.experimental.pallas import tpu as pltpu
from jax.sharding import PartitionSpec as P

SLOTS = 2
VARS = 4
FIELDS = 8
SWEEPS = 4

COEFF_X = 0.35
COEFF_Y = 0.12
CENTRE = 1.0 - 2.0 * COEFF_X - 2.0 * COEFF_Y
RATIO = COEFF_Y / COEFF_X

LANES = 128
TILE = 8
HALF = 16
VMEM_BYTES = 40 * 2**20
PREPARE_FLOPS = 10**10


def kernel_call(body, out_shape, scratch, flops, name, outside={}):
    def call(*args):
        spaces = [outside.get(i, pltpu.VMEM) for i in range(len(args))]
        return pl.pallas_call(
            body,
            out_shape=out_shape,
            in_specs=[pl.BlockSpec(memory_space=space) for space in spaces],
            out_specs=jax.tree.map(lambda _: pl.BlockSpec(memory_space=pltpu.VMEM), out_shape),
            scratch_shapes=scratch,
            compiler_params=pltpu.CompilerParams(vmem_limit_bytes=VMEM_BYTES),
            cost_estimate=pl.CostEstimate(flops=flops, bytes_accessed=1024, transcendentals=0),
            name=name,
        )(*args)

    return call


def lane_masks():
    lane = lax.broadcasted_iota(jnp.int32, (TILE, LANES), 1)
    return lane == 0, lane == LANES - 1


def top_half():
    return lax.broadcasted_iota(jnp.int32, (TILE, LANES), 0) < TILE // 2


def cols(j):
    return pl.ds(j * LANES, LANES)


def sides(values, first, last):
    before = [pltpu.roll(v, 1, 1) for v in values]
    after = [pltpu.roll(v, LANES - 1, 1) for v in values]
    zero = jnp.zeros_like(values[0])
    count = len(values)
    sums = []
    for j in range(count):
        left = jnp.where(first, before[j - 1] if j else zero, before[j])
        right = jnp.where(last, after[j + 1] if j + 1 < count else zero, after[j])
        sums.append(left + right)
    return sums


def fields_of(local, own):
    shares = VARS // own
    mem = lax.axis_index("mem")
    slot, share = mem // shares, mem % shares
    slot = slot if local else SLOTS - 1 - slot
    return [slot * VARS + at * own + k for at in (share, shares - 1 - share) for k in range(own)]


def prepare(g_ref, counts_ref, near_g_ref, rim_ref, near_counts_ref, sem):
    rows = g_ref.shape[1]
    copies = [
        pltpu.make_async_copy(g_ref.at[:, 0:TILE], rim_ref.at[:, 0:TILE], sem.at[0]),
        pltpu.make_async_copy(g_ref.at[:, rows - TILE : rows], rim_ref.at[:, TILE : 2 * TILE], sem.at[1]),
        pltpu.make_async_copy(g_ref, near_g_ref, sem.at[2]),
        pltpu.make_async_copy(counts_ref, near_counts_ref, sem.at[3]),
    ]
    for copy in copies:
        copy.start()
    for copy in copies:
        copy.wait()


def weights_of(own, refs):
    return [(ref, k) for ref in refs for k in range(own)]


def project_edges(local, own, p_ref, *rest):
    if local:
        *g_refs, counts_ref, e_ref, o_ref, u_ref = rest
    else:
        *g_refs, _, e_ref, o_ref, u_ref = rest
    members, _, rows, ny = p_ref.shape
    even = lax.axis_index("strip") % 2 == 0
    half = top_half()
    fields = fields_of(local, own)
    grads = weights_of(own, g_refs)

    def put(row, j, top, bottom):
        e_ref[row, :, cols(j)] = jnp.where(even, bottom, top)
        o_ref[row, :, cols(j)] = jnp.where(even, top, bottom)

    if local:
        for j in range(ny // LANES):
            top = counts_ref[0:TILE, cols(j)].astype(jnp.float32)
            bottom = counts_ref[rows - TILE : rows, cols(j)].astype(jnp.float32)
            put(members // 2, j, top, pltpu.roll(bottom, TILE // 2, 0))

    def pair(q):
        for j in range(ny // LANES):
            tops, bottoms = [], []
            for m in (2 * q, 2 * q + 1):
                top = bottom = None
                for f, (g_ref, k) in zip(fields, grads):
                    low = p_ref[m, f, 0:HALF, cols(j)].astype(jnp.float32)[0:TILE]
                    high = p_ref[m, f, rows - HALF : rows, cols(j)].astype(jnp.float32)[HALF - TILE :]
                    low = low * g_ref[k, 0:TILE, cols(j)]
                    high = high * g_ref[k, g_ref.shape[1] - TILE : g_ref.shape[1], cols(j)]
                    top = low if top is None else top + low
                    bottom = high if bottom is None else bottom + high
                u_ref[m, 0:TILE, cols(j)] = top
                u_ref[m, TILE : 2 * TILE, cols(j)] = bottom
                tops.append(top)
                bottoms.append(bottom)
            top = jnp.where(half, tops[0], pltpu.roll(tops[1], TILE // 2, 0))
            bottom = jnp.where(half, pltpu.roll(bottoms[0], TILE // 2, 0), bottoms[1])
            put(q, j, top, bottom)

    pl.loop(0, members // 2)(pair)


def interior(local, p_ref, *refs):
    *g_refs, counts_ref, _, own_ref, other_ref, coef, buf_a, buf_b, total_ref = refs
    members, _, rows, ny = p_ref.shape
    own = own_ref.shape[0]
    blocks = ny // LANES
    group = buf_a.shape[0]
    first, last = lane_masks()
    fields = fields_of(local, own)
    grads = weights_of(own, g_refs)
    sums = [(own_ref, k) for k in range(own)] + [(other_ref, k) for k in range(own)]
    skip = TILE // 2
    whole = list(range(0, rows, TILE))
    kept = list(range(skip, rows - skip, TILE))
    for t in range(1, SWEEPS):
        for j in range(blocks):
            active = (counts_ref[:, cols(j)] > t).astype(jnp.float32)
            total_ref[0, j] = active
            for n, r in enumerate(kept if t == SWEEPS - 1 else whole):
                active = total_ref[0, j, r : r + TILE]
                coef[t - 1, 0, j, n * TILE : (n + 1) * TILE] = active * COEFF_X
                coef[t - 1, 1, j, n * TILE : (n + 1) * TILE] = 1.0 - active * (1.0 - CENTRE)
    zero = jnp.zeros((TILE, LANES), jnp.float32)
    for buf in (buf_a, buf_b):
        for i in range(group):
            for j in range(blocks):
                buf[i, j, 0:TILE] = zero
                buf[i, j, TILE + rows :] = zero
    total_ref[...] = jnp.zeros_like(total_ref)

    def step(s, carry):
        base = s * group
        for r in range(0, rows, HALF):
            for j in range(blocks):
                weights = [g_ref[k, r : r + HALF, cols(j)] for g_ref, k in grads]
                for i in range(group):
                    total = None
                    for f, w in zip(fields, weights):
                        term = p_ref[base + i, f, r : r + HALF, cols(j)].astype(jnp.float32) * w
                        total = term if total is None else total + term
                    buf_a[i, j, TILE + r : TILE + r + HALF] = total
        src, dst = buf_a, buf_b
        for t in range(SWEEPS):
            for n, r in enumerate(kept if t == SWEEPS - 1 else whole):
                at, to = TILE + r, TILE + n * TILE
                for i in range(group):
                    centre = [src[i, j, at : at + TILE] for j in range(blocks)]
                    lateral = sides(centre, first, last)
                    for j in range(blocks):
                        stacked = src[i, j, at - 1 : at - 1 + TILE] + src[i, j, at + 1 : at + 1 + TILE]
                        moved = stacked + RATIO * lateral[j]
                        if t == 0:
                            new = COEFF_X * moved + CENTRE * centre[j]
                        else:
                            own_row = pl.ds(n * TILE, TILE)
                            new = coef[t - 1, 0, j, own_row] * moved + coef[t - 1, 1, j, own_row] * centre[j]
                        dst[i, j, to : to + TILE] = new
            src, dst = dst, src
        for r in range(0, rows, HALF):
            for j in range(blocks):
                smooth = [src[i, j, TILE - skip + r : TILE - skip + r + HALF] for i in range(group)]
                for n, f in enumerate(fields):
                    total = total_ref[n, j, r : r + HALF]
                    for i in range(group):
                        total = total + p_ref[base + i, f, r : r + HALF, cols(j)].astype(jnp.float32) * smooth[i]
                    total_ref[n, j, r : r + HALF] = total
        return carry

    lax.fori_loop(0, members // group, step, 0)
    for n, (ref, k) in enumerate(sums):
        for j in range(blocks):
            for r in range(0, rows - TILE, TILE):
                ref[k, r : r + TILE, cols(j)] = total_ref[n, j, skip + r : skip + r + TILE]


def edges(local, p_ref, u_ref, e_ref, o_ref, ce_ref, co_ref, counts_ref, _, own_ref, other_ref, coef, buf_a, buf_b, halo):
    members, _, rows, ny = p_ref.shape
    own = own_ref.shape[0]
    blocks = ny // LANES
    first, last = lane_masks()
    half = top_half()
    even = lax.axis_index("strip") % 2 == 0
    fields = fields_of(local, own)
    sums = [(own_ref, k) for k in range(own)] + [(other_ref, k) for k in range(own)]
    crow = ce_ref.shape[0] - 1
    for j in range(blocks):
        e, o = ce_ref[crow, :, cols(j)], co_ref[crow, :, cols(j)]
        halo[j, 4:12] = jnp.where(even, o, e)
        halo[j, 24:32] = jnp.where(even, e, o)
        halo[j, 8:16] = counts_ref[0:TILE, cols(j)].astype(jnp.float32)
        halo[j, 16:24] = counts_ref[rows - TILE : rows, cols(j)].astype(jnp.float32)

        def weigh(t, to, given):
            active = (given > t).astype(jnp.float32)
            coef[t, 0, j, to : to + TILE] = active * COEFF_X
            coef[t, 1, j, to : to + TILE] = 1.0 - active * (1.0 - CENTRE)

        for to in (8, 16, 24):
            weigh(0, to, halo[j, to - 3 : to + 5])
        for t in range(1, SWEEPS - 1):
            weigh(t, 8, halo[j, 6:14])
            weigh(t, 24, halo[j, 18:26])
        weigh(SWEEPS - 1, 0, jnp.where(half, halo[j, 8:16], halo[j, 16:24]))
    own_ref[...] = jnp.zeros_like(own_ref)
    other_ref[...] = jnp.zeros_like(other_ref)
    plans = [[(5, 8), (13, 16), (21, 24)], [(9, 8), (21, 24)], [(8, 8), (24, 24)]]

    def step(q, carry):
        for j in range(blocks):
            e, o = e_ref[q, :, cols(j)], o_ref[q, :, cols(j)]
            above, below = jnp.where(even, o, e), jnp.where(even, e, o)
            buf_a[0, j, 4:12] = above
            buf_a[0, j, 24:32] = below
            buf_a[1, j, 0:8] = above
            buf_a[1, j, 20:28] = below
            for i in range(2):
                buf_a[i, j, 8:16] = u_ref[2 * q + i, 0:TILE, cols(j)]
                buf_a[i, j, 16:24] = u_ref[2 * q + i, TILE : 2 * TILE, cols(j)]
        src, dst = buf_a, buf_b
        for t in range(SWEEPS - 1):
            for at, to in plans[t]:
                weights = [[coef[t, c, j, to : to + TILE] for j in range(blocks)] for c in range(2)]
                for i in range(2):
                    centre = [src[i, j, at : at + TILE] for j in range(blocks)]
                    lateral = sides(centre, first, last)
                    for j in range(blocks):
                        stacked = src[i, j, at - 1 : at - 1 + TILE] + src[i, j, at + 1 : at + 1 + TILE]
                        moved = stacked + RATIO * lateral[j]
                        dst[i, j, to : to + TILE] = weights[0][j] * moved + weights[1][j] * centre[j]
            src, dst = dst, src

        def both(ref, i, j, shift):
            low, high = ref[i, j, 10 + shift : 18 + shift], ref[i, j, 22 + shift : 30 + shift]
            return jnp.where(half, low, high)

        t = SWEEPS - 1
        weights = [[coef[t, c, j, 0:TILE] for j in range(blocks)] for c in range(2)]
        smooth = []
        for i in range(2):
            centre = [both(src, i, j, 0) for j in range(blocks)]
            lateral = sides(centre, first, last)
            result = []
            for j in range(blocks):
                moved = both(src, i, j, -1) + both(src, i, j, 1) + RATIO * lateral[j]
                result.append(weights[0][j] * moved + weights[1][j] * centre[j])
            smooth.append(result)
        for j in range(blocks):
            for f, (ref, k) in zip(fields, sums):
                total = ref[k, :, cols(j)]
                for i in range(2):
                    low = p_ref[2 * q + i, f, 0:HALF, cols(j)].astype(jnp.float32)[0:TILE]
                    high = p_ref[2 * q + i, f, rows - HALF : rows, cols(j)].astype(jnp.float32)[HALF - TILE :]
                    total = total + jnp.where(half, low, high) * smooth[i][j]
                ref[k, :, cols(j)] = total
        return carry

    lax.fori_loop(0, members // 2, step, 0)


def finish(scale, *refs):
    inner_ref, *edge_refs, out_ref = refs
    own, rows, ny = out_ref.shape
    half = top_half()
    for k in range(own):
        for j in range(ny // LANES):
            edge = sum(ref[k, :, cols(j)] for ref in edge_refs[1:]) + edge_refs[0][k, :, cols(j)]
            parts = [edge]
            for r in range(0, rows - TILE, TILE):
                parts.append(pltpu.roll(inner_ref[k, r : r + TILE, cols(j)], TILE // 2, 0))
            parts.append(edge)
            for n in range(rows // TILE):
                out_ref[k, n * TILE : (n + 1) * TILE, cols(j)] = jnp.where(half, parts[n], parts[n + 1]) * scale


def per_device(gradient, perturbations, counts):
    members, _, rows, ny = perturbations.shape
    own = gradient.shape[0]
    mem, strips = lax.axis_size("mem"), lax.axis_size("strip")
    shares = VARS // own
    blocks = ny // LANES
    assert shares == 2 and mem == shares * SLOTS and members % 2 == 0
    scale = 1.0 / math.sqrt(members * mem * FIELDS)
    f32 = jnp.float32

    near = [(i, i ^ 1) for i in range(mem)]
    across = [(i, (i + shares) % mem) for i in range(mem)]
    cross = [(i, (i + shares) % mem ^ 1) for i in range(mem)]
    even = [(i, i ^ 1) for i in range(strips) if i ^ 1 < strips]
    odd = [(i, i + 1) for i in range(1, strips - 1, 2)]
    odd = odd + [(j, i) for i, j in odd]

    def shape(*dims):
        return jax.ShapeDtypeStruct(dims, f32)

    def window(*lead):
        return pltpu.VMEM((*lead, blocks, 40, LANES), f32)

    def call_prepare(*args):
        outs = (shape(own, rows, ny), shape(own, 2 * TILE, ny), jax.ShapeDtypeStruct((rows, ny), counts.dtype))
        stored = [pltpu.with_memory_space_constraint(x, pltpu.HBM) for x in args]
        outside = {0: pl.ANY, 1: pl.ANY}
        return kernel_call(prepare, outs, [pltpu.SemaphoreType.DMA((4,))], PREPARE_FLOPS, "prepare", outside)(*stored)

    def call_project(local, *args):
        pairs = members // 2 + (1 if local else 0)
        outs = (shape(pairs, TILE, ny), shape(pairs, TILE, ny), shape(members, 2 * TILE, ny))
        outside = {} if local else {len(args) - 1: pl.ANY}
        body = lambda *refs: project_edges(local, own, *refs)
        return kernel_call(body, outs, [], 1024, "project", outside=outside)(*args)

    def call_interior(local, *args):
        outs = (shape(own, rows - TILE, ny), shape(own, rows - TILE, ny))
        total = pltpu.VMEM((VARS, blocks, rows, LANES), f32)
        buf = pltpu.VMEM((2, blocks, rows + 2 * TILE, LANES), f32)
        coef = pltpu.VMEM((SWEEPS - 1, 2, blocks, rows, LANES), f32)
        body = lambda *refs: interior(local, *refs)
        return kernel_call(body, outs, [coef, buf, buf, total], 1024, "interior", outside={len(args) - 1: pl.ANY})(*args)

    def call_edges(local, *args):
        outs = (shape(own, TILE, ny), shape(own, TILE, ny))
        scratch = [window(SWEEPS, 2), window(2), window(2), window()]
        body = lambda *refs: edges(local, *refs)
        return kernel_call(body, outs, scratch, 1024, "edges", outside={7: pl.ANY})(*args)

    near_g, _, near_counts = call_prepare(gradient, counts)
    partner = lax.ppermute(gradient, "mem", near)
    far = lax.ppermute(gradient, "mem", across)
    far_partner = lax.ppermute(gradient, "mem", cross)

    p = perturbations
    e0, o0, u0 = call_project(True, p, near_g, partner, near_counts)
    e0 = lax.ppermute(e0, "strip", even)
    o0 = lax.ppermute(o0, "strip", odd)
    own0, other0 = call_interior(True, p, near_g, partner, near_counts, u0)

    e1, o1, u1 = call_project(False, p, far, far_partner, own0)
    e1 = lax.ppermute(e1, "strip", even)
    o1 = lax.ppermute(o1, "strip", odd)
    own1, other1 = call_interior(False, p, far, far_partner, near_counts, u1)
    eown0, eother0 = call_edges(True, p, u0, e0, o0, e0, o0, near_counts, own1)
    eown1, eother1 = call_edges(False, p, u1, e1, o1, e0, o0, near_counts, eown0)

    inner = own0 + lax.ppermute(other0, "mem", near)
    inner = inner + lax.ppermute(own1, "mem", across)
    inner = inner + lax.ppermute(other1, "mem", cross)
    enear0 = lax.ppermute(eother0, "mem", near)
    efar1 = lax.ppermute(eown1, "mem", across)
    ecross1 = lax.ppermute(eother1, "mem", cross)
    return kernel_call(
        lambda *refs: finish(scale, *refs), shape(own, rows, ny), [], 1024, "finish"
    )(inner, eown0, enear0, efar1, ecross1)


def solution(mesh):
    return jax.shard_map(
        per_device,
        mesh=mesh,
        in_specs=(P("mem", "strip", None), P("mem", None, "strip", None), P("strip", None)),
        out_specs=P("mem", "strip", None),
        check_vma=False,
    )
```

```python
import math

import jax
import jax.numpy as jnp
from jax import lax
from jax.experimental import pallas as pl
from jax.experimental.pallas import tpu as pltpu
from jax.sharding import PartitionSpec as P

SLOTS = 2
VARS = 4
FIELDS = 8
SWEEPS = 4

COEFF_X = 0.35
COEFF_Y = 0.12
CENTRE = 1.0 - 2.0 * COEFF_X - 2.0 * COEFF_Y
RATIO = COEFF_Y / COEFF_X

LANES = 128
TILE = 8
HALF = 16
VMEM_BYTES = 40 * 2**20
PREPARE_FLOPS = 10**10


def kernel_call(body, out_shape, scratch, flops, name, outside={}):
    def call(*args):
        spaces = [outside.get(i, pltpu.VMEM) for i in range(len(args))]
        return pl.pallas_call(
            body,
            out_shape=out_shape,
            in_specs=[pl.BlockSpec(memory_space=space) for space in spaces],
            out_specs=jax.tree.map(lambda _: pl.BlockSpec(memory_space=pltpu.VMEM), out_shape),
            scratch_shapes=scratch,
            compiler_params=pltpu.CompilerParams(vmem_limit_bytes=VMEM_BYTES),
            cost_estimate=pl.CostEstimate(flops=flops, bytes_accessed=1024, transcendentals=0),
            name=name,
        )(*args)

    return call


def lane_masks():
    lane = lax.broadcasted_iota(jnp.int32, (TILE, LANES), 1)
    return lane == 0, lane == LANES - 1


def top_half():
    return lax.broadcasted_iota(jnp.int32, (TILE, LANES), 0) < TILE // 2


def cols(j):
    return pl.ds(j * LANES, LANES)


def sides(values, first, last):
    zero = jnp.zeros_like(values[0])
    count = len(values)
    sums = []
    for j in range(count):
        left = jnp.where(last, values[j - 1] if j else zero, values[j])
        right = jnp.where(first, values[j + 1] if j + 1 < count else zero, values[j])
        sums.append(pltpu.roll(left, 1, 1) + pltpu.roll(right, LANES - 1, 1))
    return sums


def fields_of(local, own):
    shares = VARS // own
    mem = lax.axis_index("mem")
    slot, share = mem // shares, mem % shares
    slot = slot if local else SLOTS - 1 - slot
    return [slot * VARS + at * own + k for at in (share, shares - 1 - share) for k in range(own)]


def prepare(g_ref, counts_ref, near_g_ref, near_counts_ref, sem):
    copies = [
        pltpu.make_async_copy(g_ref, near_g_ref, sem.at[0]),
        pltpu.make_async_copy(counts_ref, near_counts_ref, sem.at[1]),
    ]
    for copy in copies:
        copy.start()
    for copy in copies:
        copy.wait()


def weights_of(own, refs):
    return [(ref, k) for ref in refs for k in range(own)]


def project_edges(local, own, p_ref, *rest):
    if local:
        *g_refs, counts_ref, e_ref, o_ref = rest
    else:
        *g_refs, _, e_ref, o_ref = rest
    members, _, rows, ny = p_ref.shape
    even = lax.axis_index("strip") % 2 == 0
    half = top_half()
    fields = fields_of(local, own)
    grads = weights_of(own, g_refs)

    def put(row, j, top, bottom):
        e_ref[row, :, cols(j)] = jnp.where(even, bottom, top)
        o_ref[row, :, cols(j)] = jnp.where(even, top, bottom)

    if local:
        for j in range(ny // LANES):
            top = counts_ref[0:TILE, cols(j)].astype(jnp.float32)
            bottom = counts_ref[rows - TILE : rows, cols(j)].astype(jnp.float32)
            put(members // 2, j, top, pltpu.roll(bottom, TILE // 2, 0))

    def pair(q):
        for j in range(ny // LANES):
            tops, bottoms = [], []
            for m in (2 * q, 2 * q + 1):
                top = bottom = None
                for f, (g_ref, k) in zip(fields, grads):
                    low = p_ref[m, f, 0:HALF, cols(j)].astype(jnp.float32)[0:TILE]
                    high = p_ref[m, f, rows - HALF : rows, cols(j)].astype(jnp.float32)[HALF - TILE :]
                    low = low * g_ref[k, 0:TILE, cols(j)]
                    high = high * g_ref[k, g_ref.shape[1] - TILE : g_ref.shape[1], cols(j)]
                    top = low if top is None else top + low
                    bottom = high if bottom is None else bottom + high
                tops.append(top)
                bottoms.append(bottom)
            top = jnp.where(half, tops[0], pltpu.roll(tops[1], TILE // 2, 0))
            bottom = jnp.where(half, pltpu.roll(bottoms[0], TILE // 2, 0), bottoms[1])
            put(q, j, top, bottom)

    pl.loop(0, members // 2)(pair)


def interior(local, p_ref, *refs):
    if local:
        *g_refs, counts_ref, _, own_ref, other_ref, kept_ref, coef, buf_a, buf_b, total_ref = refs
    else:
        *g_refs, coef, _, own_ref, other_ref, kept_ref, buf_a, buf_b, total_ref = refs
    members, _, rows, ny = p_ref.shape
    own = own_ref.shape[0]
    blocks = ny // LANES
    group = buf_a.shape[0]
    first, last = lane_masks()
    half = top_half()
    fields = fields_of(local, own)
    grads = weights_of(own, g_refs)
    sums = [(own_ref, k) for k in range(own)] + [(other_ref, k) for k in range(own)]
    skip = TILE // 2
    whole = list(range(0, rows, TILE))
    kept = list(range(skip, rows - skip, TILE))
    for t in range(1, SWEEPS if local else 1):
        for j in range(blocks):
            total_ref[0, j] = (counts_ref[:, cols(j)] > t).astype(jnp.float32)
            for n, r in enumerate(kept if t == SWEEPS - 1 else whole):
                active = total_ref[0, j, r : r + TILE]
                coef[t - 1, 0, j, n * TILE : (n + 1) * TILE] = active * COEFF_X
                coef[t - 1, 1, j, n * TILE : (n + 1) * TILE] = 1.0 - active * (1.0 - CENTRE)
    zero = jnp.zeros((TILE, LANES), jnp.float32)
    for buf in (buf_a, buf_b):
        for i in range(group):
            for j in range(blocks):
                buf[i, j, 0:TILE] = zero
                buf[i, j, TILE + rows :] = zero
    total_ref[...] = jnp.zeros_like(total_ref)

    def step(s, carry):
        base = s * group
        for r in range(0, rows, HALF):
            for j in range(blocks):
                weights = [g_ref[k, r : r + HALF, cols(j)] for g_ref, k in grads]
                for i in range(group):
                    total = None
                    for f, w in zip(fields, weights):
                        term = p_ref[base + i, f, r : r + HALF, cols(j)].astype(jnp.float32) * w
                        total = term if total is None else total + term
                    buf_a[i, j, TILE + r : TILE + r + HALF] = total
        src, dst = buf_a, buf_b
        for t in range(SWEEPS):
            for i in range(group):
                for j in range(blocks):
                    low, high = TILE + t, rows - t
                    tile = jnp.where(half, src[i, j, low : low + TILE], src[i, j, high : high + TILE])
                    kept_ref[base + i, t * TILE : (t + 1) * TILE, cols(j)] = tile
            for n, r in enumerate(kept if t == SWEEPS - 1 else whole):
                at, to = TILE + r, TILE + n * TILE
                for i in range(group):
                    centre = [src[i, j, at : at + TILE] for j in range(blocks)]
                    lateral = sides(centre, first, last)
                    for j in range(blocks):
                        stacked = src[i, j, at - 1 : at - 1 + TILE] + src[i, j, at + 1 : at + 1 + TILE]
                        moved = stacked + RATIO * lateral[j]
                        if t == 0:
                            new = COEFF_X * moved + CENTRE * centre[j]
                        else:
                            own_row = pl.ds(n * TILE, TILE)
                            new = coef[t - 1, 0, j, own_row] * moved + coef[t - 1, 1, j, own_row] * centre[j]
                        dst[i, j, to : to + TILE] = new
            src, dst = dst, src
        for r in range(0, rows, HALF):
            for j in range(blocks):
                smooth = [src[i, j, TILE - skip + r : TILE - skip + r + HALF] for i in range(group)]
                for n, f in enumerate(fields):
                    total = total_ref[n, j, r : r + HALF]
                    for i in range(group):
                        total = total + p_ref[base + i, f, r : r + HALF, cols(j)].astype(jnp.float32) * smooth[i]
                    total_ref[n, j, r : r + HALF] = total
        return carry

    lax.fori_loop(0, members // group, step, 0)
    for n, (ref, k) in enumerate(sums):
        for j in range(blocks):
            for r in range(0, rows - TILE, TILE):
                ref[k, r : r + TILE, cols(j)] = total_ref[n, j, skip + r : skip + r + TILE]


def edges(local, p_ref, kept_ref, e_ref, o_ref, *refs):
    if local:
        counts_ref, own_ref, other_ref, coef, win_a, win_b, halo = refs
    else:
        coef, _, own_ref, other_ref, win_a, win_b = refs
    members, _, rows, ny = p_ref.shape
    own = own_ref.shape[0]
    blocks = ny // LANES
    first, last = lane_masks()
    half = top_half()
    even = lax.axis_index("strip") % 2 == 0
    fields = fields_of(local, own)
    sums = [(own_ref, k) for k in range(own)] + [(other_ref, k) for k in range(own)]
    start = TILE

    def sent(q, j):
        e, o = e_ref[q, :, cols(j)], o_ref[q, :, cols(j)]
        return jnp.where(even, o, e), jnp.where(even, e, o)

    def merged(ref, low, high):
        return jnp.where(half, ref[low : low + TILE], ref[high : high + TILE])

    if local:
        for j in range(blocks):
            above, below = sent(members // 2, j)
            halo[j, 4:12] = above
            halo[j, 24:32] = below
            halo[j, 8:16] = counts_ref[0:TILE, cols(j)].astype(jnp.float32)
            halo[j, 16:24] = counts_ref[rows - TILE : rows, cols(j)].astype(jnp.float32)
            for t in range(SWEEPS):
                active = (merged(halo.at[j], 5 + t, 19 - t) > t).astype(jnp.float32)
                coef[t, 0, j] = active * COEFF_X
                coef[t, 1, j] = 1.0 - active * (1.0 - CENTRE)
    own_ref[...] = jnp.zeros_like(own_ref)
    other_ref[...] = jnp.zeros_like(other_ref)

    def step(q, carry):
        for j in range(blocks):
            above, below = sent(q, j)
            win_a[0, j, start : start + TILE] = above
            win_a[0, j, start + 12 : start + 20] = below
            win_a[1, j, start - 4 : start + 4] = above
            win_a[1, j, start + 8 : start + 16] = below
            for i in range(2):
                win_a[i, j, start + 4 : start + 12] = kept_ref[2 * q + i, 0:TILE, cols(j)]
        src, dst = win_a, win_b
        smooth = [[], []]
        for t in range(SWEEPS):
            weights = [[coef[t, c, j] for j in range(blocks)] for c in range(2)]
            for i in range(2):
                centre = [merged(src.at[i, j], start + 1, start + 7) for j in range(blocks)]
                lateral = sides(centre, first, last)
                for j in range(blocks):
                    stacked = merged(src.at[i, j], start, start + 6) + merged(src.at[i, j], start + 2, start + 8)
                    new = weights[0][j] * (stacked + RATIO * lateral[j]) + weights[1][j] * centre[j]
                    if t == SWEEPS - 1:
                        smooth[i].append(new)
                    else:
                        dst[i, j, start : start + TILE] = new
                        dst[i, j, start + 8 : start + 16] = new
                        dst[i, j, start + 4 : start + 12] = kept_ref[2 * q + i, (t + 1) * TILE : (t + 2) * TILE, cols(j)]
            src, dst = dst, src
        for j in range(blocks):
            for f, (ref, k) in zip(fields, sums):
                total = ref[k, :, cols(j)]
                for i in range(2):
                    low = p_ref[2 * q + i, f, 0:HALF, cols(j)].astype(jnp.float32)[0:TILE]
                    high = p_ref[2 * q + i, f, rows - HALF : rows, cols(j)].astype(jnp.float32)[HALF - TILE :]
                    total = total + jnp.where(half, low, high) * smooth[i][j]
                ref[k, :, cols(j)] = total
        return carry

    lax.fori_loop(0, members // 2, step, 0)


def finish(scale, *refs):
    inner_ref, *edge_refs, out_ref = refs
    own, rows, ny = out_ref.shape
    half = top_half()
    for k in range(own):
        for j in range(ny // LANES):
            edge = sum(ref[k, :, cols(j)] for ref in edge_refs[1:]) + edge_refs[0][k, :, cols(j)]
            parts = [edge]
            for r in range(0, rows - TILE, TILE):
                parts.append(pltpu.roll(inner_ref[k, r : r + TILE, cols(j)], TILE // 2, 0))
            parts.append(edge)
            for n in range(rows // TILE):
                out_ref[k, n * TILE : (n + 1) * TILE, cols(j)] = jnp.where(half, parts[n], parts[n + 1]) * scale


def per_device(gradient, perturbations, counts):
    members, _, rows, ny = perturbations.shape
    own = gradient.shape[0]
    mem, strips = lax.axis_size("mem"), lax.axis_size("strip")
    shares = VARS // own
    blocks = ny // LANES
    assert shares == 2 and mem == shares * SLOTS and members % 2 == 0
    scale = 1.0 / math.sqrt(members * mem * FIELDS)
    f32 = jnp.float32

    near = [(i, i ^ 1) for i in range(mem)]
    across = [(i, (i + shares) % mem) for i in range(mem)]
    cross = [(i, (i + shares) % mem ^ 1) for i in range(mem)]
    even = [(i, i ^ 1) for i in range(strips) if i ^ 1 < strips]
    odd = [(i, i + 1) for i in range(1, strips - 1, 2)]
    odd = odd + [(j, i) for i, j in odd]

    def shape(*dims):
        return jax.ShapeDtypeStruct(dims, f32)

    def window(*lead):
        return pltpu.VMEM((*lead, blocks, 4 * TILE, LANES), f32)

    def call_prepare(*args):
        outs = (shape(own, rows, ny), jax.ShapeDtypeStruct((rows, ny), counts.dtype))
        stored = [pltpu.with_memory_space_constraint(x, pltpu.HBM) for x in args]
        outside = {0: pl.ANY, 1: pl.ANY}
        return kernel_call(prepare, outs, [pltpu.SemaphoreType.DMA((2,))], PREPARE_FLOPS, "prepare", outside)(*stored)

    def call_project(local, *args):
        pairs = members // 2 + (1 if local else 0)
        outs = (shape(pairs, TILE, ny), shape(pairs, TILE, ny))
        outside = {} if local else {len(args) - 1: pl.ANY}
        body = lambda *refs: project_edges(local, own, *refs)
        return kernel_call(body, outs, [], 1024, "project", outside=outside)(*args)

    def call_interior(local, *args):
        total = pltpu.VMEM((VARS, blocks, rows, LANES), f32)
        buf = pltpu.VMEM((2, blocks, rows + 2 * TILE, LANES), f32)
        outs = (shape(own, rows - TILE, ny), shape(own, rows - TILE, ny), shape(members, SWEEPS * TILE, ny))
        if local:
            outs = outs + (shape(SWEEPS - 1, 2, blocks, rows, LANES),)
        body = lambda *refs: interior(local, *refs)
        return kernel_call(body, outs, [buf, buf, total], 1024, "interior", outside={len(args) - 1: pl.ANY})(*args)

    def call_edges(local, *args):
        outs = (shape(own, TILE, ny), shape(own, TILE, ny))
        scratch = [window(2), window(2)]
        if local:
            outs, scratch = outs + (shape(SWEEPS, 2, blocks, TILE, LANES),), scratch + [window()]
        body = lambda *refs: edges(local, *refs)
        outside = {} if local else {len(args) - 1: pl.ANY}
        return kernel_call(body, outs, scratch, 1024, "edges", outside=outside)(*args)

    near_g, near_counts = call_prepare(gradient, counts)
    partner = lax.ppermute(gradient, "mem", near)
    far = lax.ppermute(gradient, "mem", across)
    far_partner = lax.ppermute(gradient, "mem", cross)

    p = perturbations
    e0, o0 = call_project(True, p, near_g, partner, near_counts)
    own0, other0, kept0, inner_coef = call_interior(True, p, near_g, partner, near_counts, e0)
    e0 = lax.ppermute(e0, "strip", even)
    o0 = lax.ppermute(o0, "strip", odd)

    e1, o1 = call_project(False, p, far, far_partner, own0)
    own1, other1, kept1 = call_interior(False, p, far, far_partner, inner_coef, e1)
    e1 = lax.ppermute(e1, "strip", even)
    o1 = lax.ppermute(o1, "strip", odd)
    eown0, eother0, edge_coef = call_edges(True, p, kept0, e0, o0, near_counts)
    eown1, eother1 = call_edges(False, p, kept1, e1, o1, edge_coef, eown0)

    inner = own0 + lax.ppermute(other0, "mem", near)
    inner = inner + lax.ppermute(own1, "mem", across)
    inner = inner + lax.ppermute(other1, "mem", cross)
    enear0 = lax.ppermute(eother0, "mem", near)
    efar1 = lax.ppermute(eown1, "mem", across)
    ecross1 = lax.ppermute(eother1, "mem", cross)
    return kernel_call(
        lambda *refs: finish(scale, *refs), shape(own, rows, ny), [], 1024, "finish"
    )(inner, eown0, enear0, efar1, ecross1)


def solution(mesh):
    return jax.shard_map(
        per_device,
        mesh=mesh,
        in_specs=(P("mem", "strip", None), P("mem", None, "strip", None), P("strip", None)),
        out_specs=P("mem", "strip", None),
        check_vma=False,
    )
```

```python
import math

import jax
import jax.numpy as jnp
from jax import lax
from jax.experimental import pallas as pl
from jax.experimental.pallas import tpu as pltpu
from jax.sharding import PartitionSpec as P

SLOTS = 2
VARS = 4
FIELDS = 8
SWEEPS = 4

COEFF_X = 0.35
COEFF_Y = 0.12
CENTRE = 1.0 - 2.0 * COEFF_X - 2.0 * COEFF_Y
RATIO = COEFF_Y / COEFF_X

LANES = 128
TILE = 8
HALF = 16
VMEM_BYTES = 40 * 2**20
PREPARE_FLOPS = 10**10
EDGE_GROUP = 8
INNER_GROUP = 2


def kernel_call(body, out_shape, scratch, flops, name, outside={}):
    def call(*args):
        spaces = [outside.get(i, pltpu.VMEM) for i in range(len(args))]
        return pl.pallas_call(
            body,
            out_shape=out_shape,
            in_specs=[pl.BlockSpec(memory_space=space) for space in spaces],
            out_specs=jax.tree.map(lambda _: pl.BlockSpec(memory_space=pltpu.VMEM), out_shape),
            scratch_shapes=scratch,
            compiler_params=pltpu.CompilerParams(vmem_limit_bytes=VMEM_BYTES),
            cost_estimate=pl.CostEstimate(flops=flops, bytes_accessed=1024, transcendentals=0),
            name=name,
        )(*args)

    return call


def lane_masks():
    lane = lax.broadcasted_iota(jnp.int32, (TILE, LANES), 1)
    return lane == 0, lane == LANES - 1


def top_half():
    return lax.broadcasted_iota(jnp.int32, (TILE, LANES), 0) < TILE // 2


def cols(j):
    return pl.ds(j * LANES, LANES)


def sides(values, first, last):
    zero = jnp.zeros_like(values[0])
    count = len(values)
    sums = []
    for j in range(count):
        left = jnp.where(last, values[j - 1] if j else zero, values[j])
        right = jnp.where(first, values[j + 1] if j + 1 < count else zero, values[j])
        sums.append(pltpu.roll(left, 1, 1) + pltpu.roll(right, LANES - 1, 1))
    return sums


def fields_of(local, own):
    shares = VARS // own
    mem = lax.axis_index("mem")
    slot, share = mem // shares, mem % shares
    slot = slot if local else SLOTS - 1 - slot
    return [slot * VARS + at * own + k for at in (share, shares - 1 - share) for k in range(own)]


def prepare(g_ref, counts_ref, near_g_ref, rim_ref, near_counts_ref, sem):
    rows = g_ref.shape[1]
    copies = [
        pltpu.make_async_copy(g_ref.at[:, 0:TILE], rim_ref.at[:, 0:TILE], sem.at[0]),
        pltpu.make_async_copy(g_ref.at[:, rows - TILE : rows], rim_ref.at[:, TILE : 2 * TILE], sem.at[1]),
        pltpu.make_async_copy(g_ref, near_g_ref, sem.at[2]),
        pltpu.make_async_copy(counts_ref, near_counts_ref, sem.at[3]),
    ]
    for copy in copies:
        copy.start()
    for copy in copies:
        copy.wait()


def weights_of(own, refs):
    return [(ref, k) for ref in refs for k in range(own)]


def project_edges(local, own, p_ref, *rest):
    if local:
        *g_refs, counts_ref, e_ref, o_ref = rest
    else:
        *g_refs, _, e_ref, o_ref = rest
    members, _, rows, ny = p_ref.shape
    even = lax.axis_index("strip") % 2 == 0
    half = top_half()
    fields = fields_of(local, own)
    grads = weights_of(own, g_refs)

    def put(row, j, top, bottom):
        e_ref[row, :, cols(j)] = jnp.where(even, bottom, top)
        o_ref[row, :, cols(j)] = jnp.where(even, top, bottom)

    if local:
        for j in range(ny // LANES):
            top = counts_ref[0:TILE, cols(j)].astype(jnp.float32)
            bottom = counts_ref[rows - TILE : rows, cols(j)].astype(jnp.float32)
            put(members // 2, j, top, pltpu.roll(bottom, TILE // 2, 0))

    def pair(q):
        for j in range(ny // LANES):
            tops, bottoms = [], []
            for m in (2 * q, 2 * q + 1):
                top = bottom = None
                for f, (g_ref, k) in zip(fields, grads):
                    low = p_ref[m, f, 0:HALF, cols(j)].astype(jnp.float32)[0:TILE]
                    high = p_ref[m, f, rows - HALF : rows, cols(j)].astype(jnp.float32)[HALF - TILE :]
                    low = low * g_ref[k, 0:TILE, cols(j)]
                    high = high * g_ref[k, g_ref.shape[1] - TILE : g_ref.shape[1], cols(j)]
                    top = low if top is None else top + low
                    bottom = high if bottom is None else bottom + high
                tops.append(top)
                bottoms.append(bottom)
            top = jnp.where(half, tops[0], pltpu.roll(tops[1], TILE // 2, 0))
            bottom = jnp.where(half, pltpu.roll(bottoms[0], TILE // 2, 0), bottoms[1])
            put(q, j, top, bottom)

    pl.loop(0, members // 2)(pair)


def interior(local, p_ref, *refs):
    if local:
        *g_refs, counts_ref, _, own_ref, other_ref, kept_ref, coef, buf_a, buf_b, total_ref = refs
    else:
        *g_refs, coef, _, own_ref, other_ref, kept_ref, buf_a, buf_b, total_ref = refs
    members, _, rows, ny = p_ref.shape
    own = own_ref.shape[0]
    blocks = ny // LANES
    group = buf_a.shape[0]
    first, last = lane_masks()
    half = top_half()
    fields = fields_of(local, own)
    grads = weights_of(own, g_refs)
    sums = [(own_ref, k) for k in range(own)] + [(other_ref, k) for k in range(own)]
    skip = TILE // 2
    whole = list(range(0, rows, TILE))
    kept = list(range(skip, rows - skip, TILE))
    for t in range(1, SWEEPS if local else 1):
        for j in range(blocks):
            total_ref[0, j] = (counts_ref[:, cols(j)] > t).astype(jnp.float32)
            for n, r in enumerate(kept if t == SWEEPS - 1 else whole):
                active = total_ref[0, j, r : r + TILE]
                coef[t - 1, 0, j, n * TILE : (n + 1) * TILE] = active * COEFF_X
                coef[t - 1, 1, j, n * TILE : (n + 1) * TILE] = 1.0 - active * (1.0 - CENTRE)
    zero = jnp.zeros((TILE, LANES), jnp.float32)
    for buf in (buf_a, buf_b):
        for i in range(group):
            for j in range(blocks):
                buf[i, j, 0:TILE] = zero
                buf[i, j, TILE + rows :] = zero
    total_ref[...] = jnp.zeros_like(total_ref)

    def step(s, carry):
        base = s * group
        for r in range(0, rows, HALF):
            for j in range(blocks):
                weights = [g_ref[k, r : r + HALF, cols(j)] for g_ref, k in grads]
                for i in range(group):
                    total = None
                    for f, w in zip(fields, weights):
                        term = p_ref[base + i, f, r : r + HALF, cols(j)].astype(jnp.float32) * w
                        total = term if total is None else total + term
                    buf_a[i, j, TILE + r : TILE + r + HALF] = total
        src, dst = buf_a, buf_b
        for t in range(SWEEPS):
            for i in range(group):
                for j in range(blocks):
                    low, high = TILE + t, rows - t
                    tile = jnp.where(half, src[i, j, low : low + TILE], src[i, j, high : high + TILE])
                    kept_ref[base + i, t * TILE : (t + 1) * TILE, cols(j)] = tile
            for n, r in enumerate(kept if t == SWEEPS - 1 else whole):
                at, to = TILE + r, TILE + n * TILE
                for i in range(group):
                    centre = [src[i, j, at : at + TILE] for j in range(blocks)]
                    lateral = sides(centre, first, last)
                    for j in range(blocks):
                        stacked = src[i, j, at - 1 : at - 1 + TILE] + src[i, j, at + 1 : at + 1 + TILE]
                        moved = stacked + RATIO * lateral[j]
                        if t == 0:
                            new = COEFF_X * moved + CENTRE * centre[j]
                        else:
                            own_row = pl.ds(n * TILE, TILE)
                            new = coef[t - 1, 0, j, own_row] * moved + coef[t - 1, 1, j, own_row] * centre[j]
                        dst[i, j, to : to + TILE] = new
            src, dst = dst, src
        for r in range(0, rows, HALF):
            for j in range(blocks):
                smooth = [src[i, j, TILE - skip + r : TILE - skip + r + HALF] for i in range(group)]
                for n, f in enumerate(fields):
                    total = total_ref[n, j, r : r + HALF]
                    for i in range(group):
                        total = total + p_ref[base + i, f, r : r + HALF, cols(j)].astype(jnp.float32) * smooth[i]
                    total_ref[n, j, r : r + HALF] = total
        return carry

    lax.fori_loop(0, members // group, step, 0)
    for n, (ref, k) in enumerate(sums):
        for j in range(blocks):
            for r in range(0, rows - TILE, TILE):
                ref[k, r : r + TILE, cols(j)] = total_ref[n, j, skip + r : skip + r + TILE]


def edges(local, p_ref, kept_ref, e_ref, o_ref, *refs):
    if local:
        counts_ref, own_ref, other_ref, coef, win_a, win_b, halo = refs
    else:
        coef, _, own_ref, other_ref, win_a, win_b = refs
    members, _, rows, ny = p_ref.shape
    own = own_ref.shape[0]
    blocks = ny // LANES
    first, last = lane_masks()
    half = top_half()
    even = lax.axis_index("strip") % 2 == 0
    fields = fields_of(local, own)
    sums = [(own_ref, k) for k in range(own)] + [(other_ref, k) for k in range(own)]
    start = TILE

    def sent(q, j):
        e, o = e_ref[q, :, cols(j)], o_ref[q, :, cols(j)]
        return jnp.where(even, o, e), jnp.where(even, e, o)

    def merged(ref, low, high):
        return jnp.where(half, ref[low : low + TILE], ref[high : high + TILE])

    if local:
        for j in range(blocks):
            above, below = sent(members // 2, j)
            halo[j, 4:12] = above
            halo[j, 24:32] = below
            halo[j, 8:16] = counts_ref[0:TILE, cols(j)].astype(jnp.float32)
            halo[j, 16:24] = counts_ref[rows - TILE : rows, cols(j)].astype(jnp.float32)
            for t in range(SWEEPS):
                active = (merged(halo.at[j], 5 + t, 19 - t) > t).astype(jnp.float32)
                coef[t, 0, j] = active * COEFF_X
                coef[t, 1, j] = 1.0 - active * (1.0 - CENTRE)
    own_ref[...] = jnp.zeros_like(own_ref)
    other_ref[...] = jnp.zeros_like(other_ref)

    group = win_a.shape[0]

    def step(s, carry):
        base = s * group
        for j in range(blocks):
            for i in range(0, group, 2):
                above, below = sent(s * (group // 2) + i // 2, j)
                win_a[i, j, start : start + TILE] = above
                win_a[i, j, start + 12 : start + 20] = below
                win_a[i + 1, j, start - 4 : start + 4] = above
                win_a[i + 1, j, start + 8 : start + 16] = below
            for i in range(group):
                win_a[i, j, start + 4 : start + 12] = kept_ref[base + i, 0:TILE, cols(j)]
        src, dst = win_a, win_b
        smooth = [[] for i in range(group)]
        for t in range(SWEEPS):
            weights = [[coef[t, c, j] for j in range(blocks)] for c in range(2)]
            for i in range(group):
                centre = [merged(src.at[i, j], start + 1, start + 7) for j in range(blocks)]
                lateral = sides(centre, first, last)
                for j in range(blocks):
                    stacked = merged(src.at[i, j], start, start + 6) + merged(src.at[i, j], start + 2, start + 8)
                    new = weights[0][j] * (stacked + RATIO * lateral[j]) + weights[1][j] * centre[j]
                    if t == SWEEPS - 1:
                        smooth[i].append(new)
                    else:
                        dst[i, j, start : start + TILE] = new
                        dst[i, j, start + 8 : start + 16] = new
                        dst[i, j, start + 4 : start + 12] = kept_ref[base + i, (t + 1) * TILE : (t + 2) * TILE, cols(j)]
            src, dst = dst, src
        for j in range(blocks):
            for f, (ref, k) in zip(fields, sums):
                total = ref[k, :, cols(j)]
                for i in range(group):
                    low = p_ref[base + i, f, 0:HALF, cols(j)].astype(jnp.float32)[0:TILE]
                    high = p_ref[base + i, f, rows - HALF : rows, cols(j)].astype(jnp.float32)[HALF - TILE :]
                    total = total + jnp.where(half, low, high) * smooth[i][j]
                ref[k, :, cols(j)] = total
        return carry

    lax.fori_loop(0, members // group, step, 0)


def relay(*refs):
    count = len(refs) // 2
    for ref, out_ref in zip(refs[:count], refs[count + 1 :]):
        out_ref[...] = ref[...]


def finish(scale, *refs):
    inner_ref, *edge_refs, out_ref = refs
    own, rows, ny = out_ref.shape
    half = top_half()
    for k in range(own):
        for j in range(ny // LANES):
            edge = sum(ref[k, :, cols(j)] for ref in edge_refs[1:]) + edge_refs[0][k, :, cols(j)]
            parts = [edge]
            for r in range(0, rows - TILE, TILE):
                parts.append(pltpu.roll(inner_ref[k, r : r + TILE, cols(j)], TILE // 2, 0))
            parts.append(edge)
            for n in range(rows // TILE):
                out_ref[k, n * TILE : (n + 1) * TILE, cols(j)] = jnp.where(half, parts[n], parts[n + 1]) * scale


def per_device(gradient, perturbations, counts):
    members, _, rows, ny = perturbations.shape
    own = gradient.shape[0]
    mem, strips = lax.axis_size("mem"), lax.axis_size("strip")
    shares = VARS // own
    blocks = ny // LANES
    assert shares == 2 and mem == shares * SLOTS and members % 2 == 0
    scale = 1.0 / math.sqrt(members * mem * FIELDS)
    f32 = jnp.float32

    near = [(i, i ^ 1) for i in range(mem)]
    across = [(i, (i + shares) % mem) for i in range(mem)]
    cross = [(i, (i + shares) % mem ^ 1) for i in range(mem)]
    even = [(i, i ^ 1) for i in range(strips) if i ^ 1 < strips]
    odd = [(i, i + 1) for i in range(1, strips - 1, 2)]
    odd = odd + [(j, i) for i, j in odd]

    def shape(*dims):
        return jax.ShapeDtypeStruct(dims, f32)

    def window(*lead):
        return pltpu.VMEM((*lead, blocks, 4 * TILE, LANES), f32)

    def call_prepare(*args):
        outs = (shape(own, rows, ny), shape(own, 2 * TILE, ny), jax.ShapeDtypeStruct((rows, ny), counts.dtype))
        stored = [pltpu.with_memory_space_constraint(x, pltpu.HBM) for x in args]
        outside = {0: pl.ANY, 1: pl.ANY}
        return kernel_call(prepare, outs, [pltpu.SemaphoreType.DMA((4,))], PREPARE_FLOPS, "prepare", outside)(*stored)

    def call_project(local, *args):
        pairs = members // 2 + (1 if local else 0)
        outs = (shape(pairs, TILE, ny), shape(pairs, TILE, ny))
        outside = {} if local else {len(args) - 1: pl.ANY}
        body = lambda *refs: project_edges(local, own, *refs)
        return kernel_call(body, outs, [], 1024, "project", outside=outside)(*args)

    def call_relay(*args):
        outs = tuple(shape(*x.shape) for x in args[:-1])
        return kernel_call(relay, outs, [], 1024, "relay", outside={len(outs): pl.ANY})(*args)

    def call_interior(local, *args):
        total = pltpu.VMEM((VARS, blocks, rows, LANES), f32)
        buf = pltpu.VMEM((INNER_GROUP, blocks, rows + 2 * TILE, LANES), f32)
        outs = (shape(own, rows - TILE, ny), shape(own, rows - TILE, ny), shape(members, SWEEPS * TILE, ny))
        if local:
            outs = outs + (shape(SWEEPS - 1, 2, blocks, rows, LANES),)
        body = lambda *refs: interior(local, *refs)
        return kernel_call(body, outs, [buf, buf, total], 1024, "interior", outside={len(args) - 1: pl.ANY})(*args)

    def call_edges(local, *args):
        outs = (shape(own, TILE, ny), shape(own, TILE, ny))
        scratch = [window(EDGE_GROUP), window(EDGE_GROUP)]
        if local:
            outs, scratch = outs + (shape(SWEEPS, 2, blocks, TILE, LANES),), scratch + [window()]
        body = lambda *refs: edges(local, *refs)
        outside = {} if local else {len(args) - 1: pl.ANY}
        return kernel_call(body, outs, scratch, 1024, "edges", outside=outside)(*args)

    near_g, rim, near_counts = call_prepare(gradient, counts)
    partner = lax.ppermute(gradient, "mem", near)
    far = lax.ppermute(gradient, "mem", across)
    far_rim = lax.ppermute(rim, "mem", cross)

    p = perturbations
    e0, o0 = call_project(True, p, near_g, partner, near_counts)
    own0, other0, kept0, inner_coef = call_interior(True, p, near_g, partner, near_counts, o0)
    e0 = lax.ppermute(e0, "strip", even)
    o0 = lax.ppermute(o0, "strip", odd)

    e1, o1 = call_project(False, p, far, far_rim, own0)
    far_partner = lax.ppermute(call_relay(far, o1)[0], "mem", near)
    own1, other1, kept1 = call_interior(False, p, far, far_partner, inner_coef, o1)
    e1 = lax.ppermute(e1, "strip", even)
    o1 = lax.ppermute(o1, "strip", odd)
    eown0, eother0, edge_coef = call_edges(True, p, kept0, e0, o0, near_counts)
    eown1, eother1 = call_edges(False, p, kept1, e1, o1, edge_coef, eown0)

    inner = own0 + lax.ppermute(other0, "mem", near)
    inner = inner + lax.ppermute(own1, "mem", across)
    inner = inner + lax.ppermute(other1, "mem", cross)
    enear0 = lax.ppermute(eother0, "mem", near)
    efar1 = lax.ppermute(eown1, "mem", across)
    ecross1 = lax.ppermute(eother1, "mem", cross)
    return kernel_call(
        lambda *refs: finish(scale, *refs), shape(own, rows, ny), [], 1024, "finish"
    )(inner, eown0, enear0, efar1, ecross1)


def solution(mesh):
    return jax.shard_map(
        per_device,
        mesh=mesh,
        in_specs=(P("mem", "strip", None), P("mem", None, "strip", None), P("strip", None)),
        out_specs=P("mem", "strip", None),
        check_vma=False,
    )
```

```python
import math

import jax
import jax.numpy as jnp
from jax import lax
from jax.experimental import pallas as pl
from jax.experimental.pallas import tpu as pltpu
from jax.sharding import PartitionSpec as P

SLOTS = 2
VARS = 4
FIELDS = 8
SWEEPS = 4

COEFF_X = 0.35
COEFF_Y = 0.12
CENTRE = 1.0 - 2.0 * COEFF_X - 2.0 * COEFF_Y
RATIO = COEFF_Y / COEFF_X

LANES = 128
TILE = 8
HALF = 16
VMEM_BYTES = 40 * 2**20
PREPARE_FLOPS = 10**10
EDGE_GROUP = 8
INNER_GROUP = 2


def kernel_call(body, out_shape, scratch, flops, name, outside={}):
    def call(*args):
        spaces = [outside.get(i, pltpu.VMEM) for i in range(len(args))]
        return pl.pallas_call(
            body,
            out_shape=out_shape,
            in_specs=[pl.BlockSpec(memory_space=space) for space in spaces],
            out_specs=jax.tree.map(lambda _: pl.BlockSpec(memory_space=pltpu.VMEM), out_shape),
            scratch_shapes=scratch,
            compiler_params=pltpu.CompilerParams(vmem_limit_bytes=VMEM_BYTES),
            cost_estimate=pl.CostEstimate(flops=flops, bytes_accessed=1024, transcendentals=0),
            name=name,
        )(*args)

    return call


def lane_masks():
    lane = lax.broadcasted_iota(jnp.int32, (TILE, LANES), 1)
    return lane == 0, lane == LANES - 1


def top_half():
    return lax.broadcasted_iota(jnp.int32, (TILE, LANES), 0) < TILE // 2


def cols(j):
    return pl.ds(j * LANES, LANES)


def sides(values, first, last):
    zero = jnp.zeros_like(values[0])
    count = len(values)
    sums = []
    for j in range(count):
        left = jnp.where(last, values[j - 1] if j else zero, values[j])
        right = jnp.where(first, values[j + 1] if j + 1 < count else zero, values[j])
        sums.append(pltpu.roll(left, 1, 1) + pltpu.roll(right, LANES - 1, 1))
    return sums


def fields_of(local, own):
    shares = VARS // own
    mem = lax.axis_index("mem")
    slot, share = mem // shares, mem % shares
    slot = slot if local else SLOTS - 1 - slot
    return [slot * VARS + at * own + k for at in (share, shares - 1 - share) for k in range(own)]


def prepare(g_ref, counts_ref, near_g_ref, rim_ref, near_counts_ref, sem):
    rows = g_ref.shape[1]
    copies = [
        pltpu.make_async_copy(g_ref.at[:, 0:TILE], rim_ref.at[:, 0:TILE], sem.at[0]),
        pltpu.make_async_copy(g_ref.at[:, rows - TILE : rows], rim_ref.at[:, TILE : 2 * TILE], sem.at[1]),
        pltpu.make_async_copy(g_ref, near_g_ref, sem.at[2]),
        pltpu.make_async_copy(counts_ref, near_counts_ref, sem.at[3]),
    ]
    for copy in copies:
        copy.start()
    for copy in copies:
        copy.wait()


def weights_of(own, refs):
    return [(ref, k) for ref in refs for k in range(own)]


def project_edges(local, own, p_ref, *rest):
    if local:
        *g_refs, counts_ref, e_ref, o_ref = rest
    else:
        *g_refs, _, e_ref, o_ref = rest
    members, _, rows, ny = p_ref.shape
    even = lax.axis_index("strip") % 2 == 0
    half = top_half()
    fields = fields_of(local, own)
    grads = weights_of(own, g_refs)

    def put(row, j, top, bottom):
        e_ref[row, :, cols(j)] = jnp.where(even, bottom, top)
        o_ref[row, :, cols(j)] = jnp.where(even, top, bottom)

    if local:
        for j in range(ny // LANES):
            top = counts_ref[0:TILE, cols(j)].astype(jnp.float32)
            bottom = counts_ref[rows - TILE : rows, cols(j)].astype(jnp.float32)
            put(members // 2, j, top, pltpu.roll(bottom, TILE // 2, 0))

    def pair(q):
        for j in range(ny // LANES):
            tops, bottoms = [], []
            for m in (2 * q, 2 * q + 1):
                top = bottom = None
                for f, (g_ref, k) in zip(fields, grads):
                    low = p_ref[m, f, 0:HALF, cols(j)].astype(jnp.float32)[0:TILE]
                    high = p_ref[m, f, rows - HALF : rows, cols(j)].astype(jnp.float32)[HALF - TILE :]
                    low = low * g_ref[k, 0:TILE, cols(j)]
                    high = high * g_ref[k, g_ref.shape[1] - TILE : g_ref.shape[1], cols(j)]
                    top = low if top is None else top + low
                    bottom = high if bottom is None else bottom + high
                tops.append(top)
                bottoms.append(bottom)
            top = jnp.where(half, tops[0], pltpu.roll(tops[1], TILE // 2, 0))
            bottom = jnp.where(half, pltpu.roll(bottoms[0], TILE // 2, 0), bottoms[1])
            put(q, j, top, bottom)

    pl.loop(0, members // 2)(pair)


def interior(local, p_ref, *refs):
    if not local:
        *g_refs, counts_ref, _, own_ref, other_ref, kept_ref, coef, buf_a, buf_b, total_ref = refs
    else:
        *g_refs, coef, _, own_ref, other_ref, kept_ref, buf_a, buf_b, total_ref = refs
    members, _, rows, ny = p_ref.shape
    own = own_ref.shape[0]
    blocks = ny // LANES
    group = buf_a.shape[0]
    first, last = lane_masks()
    half = top_half()
    fields = fields_of(local, own)
    grads = weights_of(own, g_refs)
    sums = [(own_ref, k) for k in range(own)] + [(other_ref, k) for k in range(own)]
    skip = TILE // 2
    whole = list(range(0, rows, TILE))
    kept = list(range(skip, rows - skip, TILE))
    for t in range(1, 1 if local else SWEEPS):
        for j in range(blocks):
            total_ref[0, j] = (counts_ref[:, cols(j)] > t).astype(jnp.float32)
            for n, r in enumerate(kept if t == SWEEPS - 1 else whole):
                active = total_ref[0, j, r : r + TILE]
                coef[t - 1, 0, j, n * TILE : (n + 1) * TILE] = active * COEFF_X
                coef[t - 1, 1, j, n * TILE : (n + 1) * TILE] = 1.0 - active * (1.0 - CENTRE)
    zero = jnp.zeros((TILE, LANES), jnp.float32)
    for buf in (buf_a, buf_b):
        for i in range(group):
            for j in range(blocks):
                buf[i, j, 0:TILE] = zero
                buf[i, j, TILE + rows :] = zero
    total_ref[...] = jnp.zeros_like(total_ref)

    def step(s, carry):
        base = s * group
        for r in range(0, rows, HALF):
            for j in range(blocks):
                weights = [g_ref[k, r : r + HALF, cols(j)] for g_ref, k in grads]
                for i in range(group):
                    total = None
                    for f, w in zip(fields, weights):
                        term = p_ref[base + i, f, r : r + HALF, cols(j)].astype(jnp.float32) * w
                        total = term if total is None else total + term
                    buf_a[i, j, TILE + r : TILE + r + HALF] = total
        src, dst = buf_a, buf_b
        for t in range(SWEEPS):
            for i in range(group):
                for j in range(blocks):
                    low, high = TILE + t, rows - t
                    tile = jnp.where(half, src[i, j, low : low + TILE], src[i, j, high : high + TILE])
                    kept_ref[base + i, t * TILE : (t + 1) * TILE, cols(j)] = tile
            for n, r in enumerate(kept if t == SWEEPS - 1 else whole):
                at, to = TILE + r, TILE + n * TILE
                for i in range(group):
                    centre = [src[i, j, at : at + TILE] for j in range(blocks)]
                    lateral = sides(centre, first, last)
                    for j in range(blocks):
                        stacked = src[i, j, at - 1 : at - 1 + TILE] + src[i, j, at + 1 : at + 1 + TILE]
                        moved = stacked + RATIO * lateral[j]
                        if t == 0:
                            new = COEFF_X * moved + CENTRE * centre[j]
                        else:
                            own_row = pl.ds(n * TILE, TILE)
                            new = coef[t - 1, 0, j, own_row] * moved + coef[t - 1, 1, j, own_row] * centre[j]
                        dst[i, j, to : to + TILE] = new
            src, dst = dst, src
        for r in range(0, rows, HALF):
            for j in range(blocks):
                smooth = [src[i, j, TILE - skip + r : TILE - skip + r + HALF] for i in range(group)]
                for n, f in enumerate(fields):
                    total = total_ref[n, j, r : r + HALF]
                    for i in range(group):
                        total = total + p_ref[base + i, f, r : r + HALF, cols(j)].astype(jnp.float32) * smooth[i]
                    total_ref[n, j, r : r + HALF] = total
        return carry

    lax.fori_loop(0, members // group, step, 0)
    for n, (ref, k) in enumerate(sums):
        for j in range(blocks):
            for r in range(0, rows - TILE, TILE):
                ref[k, r : r + TILE, cols(j)] = total_ref[n, j, skip + r : skip + r + TILE]


def edges(local, p_ref, kept_ref, e_ref, o_ref, *refs):
    if local:
        counts_ref, own_ref, other_ref, coef, win_a, win_b, halo = refs
    else:
        coef, _, own_ref, other_ref, win_a, win_b = refs
    members, _, rows, ny = p_ref.shape
    own = own_ref.shape[0]
    blocks = ny // LANES
    first, last = lane_masks()
    half = top_half()
    even = lax.axis_index("strip") % 2 == 0
    fields = fields_of(local, own)
    sums = [(own_ref, k) for k in range(own)] + [(other_ref, k) for k in range(own)]
    start = TILE

    def sent(q, j):
        e, o = e_ref[q, :, cols(j)], o_ref[q, :, cols(j)]
        return jnp.where(even, o, e), jnp.where(even, e, o)

    def merged(ref, low, high):
        return jnp.where(half, ref[low : low + TILE], ref[high : high + TILE])

    if local:
        for j in range(blocks):
            above, below = sent(members // 2, j)
            halo[j, 4:12] = above
            halo[j, 24:32] = below
            halo[j, 8:16] = counts_ref[0:TILE, cols(j)].astype(jnp.float32)
            halo[j, 16:24] = counts_ref[rows - TILE : rows, cols(j)].astype(jnp.float32)
            for t in range(SWEEPS):
                active = (merged(halo.at[j], 5 + t, 19 - t) > t).astype(jnp.float32)
                coef[t, 0, j] = active * COEFF_X
                coef[t, 1, j] = 1.0 - active * (1.0 - CENTRE)
    own_ref[...] = jnp.zeros_like(own_ref)
    other_ref[...] = jnp.zeros_like(other_ref)

    group = win_a.shape[0]

    def step(s, carry):
        base = s * group
        for j in range(blocks):
            for i in range(0, group, 2):
                above, below = sent(s * (group // 2) + i // 2, j)
                win_a[i, j, start : start + TILE] = above
                win_a[i, j, start + 12 : start + 20] = below
                win_a[i + 1, j, start - 4 : start + 4] = above
                win_a[i + 1, j, start + 8 : start + 16] = below
            for i in range(group):
                win_a[i, j, start + 4 : start + 12] = kept_ref[base + i, 0:TILE, cols(j)]
        src, dst = win_a, win_b
        smooth = [[] for i in range(group)]
        for t in range(SWEEPS):
            weights = [[coef[t, c, j] for j in range(blocks)] for c in range(2)]
            for i in range(group):
                centre = [merged(src.at[i, j], start + 1, start + 7) for j in range(blocks)]
                lateral = sides(centre, first, last)
                for j in range(blocks):
                    stacked = merged(src.at[i, j], start, start + 6) + merged(src.at[i, j], start + 2, start + 8)
                    new = weights[0][j] * (stacked + RATIO * lateral[j]) + weights[1][j] * centre[j]
                    if t == SWEEPS - 1:
                        smooth[i].append(new)
                    else:
                        dst[i, j, start : start + TILE] = new
                        dst[i, j, start + 8 : start + 16] = new
                        dst[i, j, start + 4 : start + 12] = kept_ref[base + i, (t + 1) * TILE : (t + 2) * TILE, cols(j)]
            src, dst = dst, src
        for j in range(blocks):
            for f, (ref, k) in zip(fields, sums):
                total = ref[k, :, cols(j)]
                for i in range(group):
                    low = p_ref[base + i, f, 0:HALF, cols(j)].astype(jnp.float32)[0:TILE]
                    high = p_ref[base + i, f, rows - HALF : rows, cols(j)].astype(jnp.float32)[HALF - TILE :]
                    total = total + jnp.where(half, low, high) * smooth[i][j]
                ref[k, :, cols(j)] = total
        return carry

    lax.fori_loop(0, members // group, step, 0)


def relay(*refs):
    count = len(refs) // 2
    for ref, out_ref in zip(refs[:count], refs[count + 1 :]):
        out_ref[...] = ref[...]


def finish(scale, *refs):
    own_ref, near_ref, inner_ref, *edge_refs, out_ref = refs
    own, rows, ny = out_ref.shape
    half = top_half()
    for k in range(own):
        for j in range(ny // LANES):
            edge = sum(ref[k, :, cols(j)] for ref in edge_refs[1:]) + edge_refs[0][k, :, cols(j)]
            parts = [edge]
            for r in range(0, rows - TILE, TILE):
                inner = own_ref[k, r : r + TILE, cols(j)] + near_ref[k, r : r + TILE, cols(j)] + inner_ref[k, r : r + TILE, cols(j)]
                parts.append(pltpu.roll(inner, TILE // 2, 0))
            parts.append(edge)
            for n in range(rows // TILE):
                out_ref[k, n * TILE : (n + 1) * TILE, cols(j)] = jnp.where(half, parts[n], parts[n + 1]) * scale


def per_device(gradient, perturbations, counts):
    members, _, rows, ny = perturbations.shape
    own = gradient.shape[0]
    mem, strips = lax.axis_size("mem"), lax.axis_size("strip")
    shares = VARS // own
    blocks = ny // LANES
    assert shares == 2 and mem == shares * SLOTS and members % 2 == 0
    scale = 1.0 / math.sqrt(members * mem * FIELDS)
    f32 = jnp.float32

    near = [(i, i ^ 1) for i in range(mem)]
    across = [(i, (i + shares) % mem) for i in range(mem)]
    cross = [(i, (i + shares) % mem ^ 1) for i in range(mem)]
    even = [(i, i ^ 1) for i in range(strips) if i ^ 1 < strips]
    odd = [(i, i + 1) for i in range(1, strips - 1, 2)]
    odd = odd + [(j, i) for i, j in odd]

    def shape(*dims):
        return jax.ShapeDtypeStruct(dims, f32)

    def window(*lead):
        return pltpu.VMEM((*lead, blocks, 4 * TILE, LANES), f32)

    def call_prepare(*args):
        outs = (shape(own, rows, ny), shape(own, 2 * TILE, ny), jax.ShapeDtypeStruct((rows, ny), counts.dtype))
        stored = [pltpu.with_memory_space_constraint(x, pltpu.HBM) for x in args]
        outside = {0: pl.ANY, 1: pl.ANY}
        return kernel_call(prepare, outs, [pltpu.SemaphoreType.DMA((4,))], PREPARE_FLOPS, "prepare", outside)(*stored)

    def call_project(local, *args):
        pairs = members // 2 + (1 if local else 0)
        outs = (shape(pairs, TILE, ny), shape(pairs, TILE, ny))
        outside = {} if local else {len(args) - 1: pl.ANY}
        body = lambda *refs: project_edges(local, own, *refs)
        return kernel_call(body, outs, [], 1024, "project", outside=outside)(*args)

    def call_relay(*args):
        outs = tuple(shape(*x.shape) for x in args[:-1])
        return kernel_call(relay, outs, [], 1024, "relay", outside={len(outs): pl.ANY})(*args)

    def call_interior(local, *args):
        total = pltpu.VMEM((VARS, blocks, rows, LANES), f32)
        buf = pltpu.VMEM((INNER_GROUP, blocks, rows + 2 * TILE, LANES), f32)
        outs = (shape(own, rows - TILE, ny), shape(own, rows - TILE, ny), shape(members, SWEEPS * TILE, ny))
        if not local:
            outs = outs + (shape(SWEEPS - 1, 2, blocks, rows, LANES),)
        body = lambda *refs: interior(local, *refs)
        return kernel_call(body, outs, [buf, buf, total], 1024, "interior", outside={len(args) - 1: pl.ANY})(*args)

    def call_edges(local, *args):
        outs = (shape(own, TILE, ny), shape(own, TILE, ny))
        scratch = [window(EDGE_GROUP), window(EDGE_GROUP)]
        if local:
            outs, scratch = outs + (shape(SWEEPS, 2, blocks, TILE, LANES),), scratch + [window()]
        body = lambda *refs: edges(local, *refs)
        outside = {} if local else {len(args) - 1: pl.ANY}
        return kernel_call(body, outs, scratch, 1024, "edges", outside=outside)(*args)

    near_g, rim, near_counts = call_prepare(gradient, counts)
    partner = lax.ppermute(gradient, "mem", near)
    far = lax.ppermute(gradient, "mem", across)
    far_rim = lax.ppermute(rim, "mem", cross)

    p = perturbations
    e0, o0 = call_project(True, p, near_g, partner, near_counts)
    e1, o1 = call_project(False, p, far, far_rim, o0)
    far_partner = lax.ppermute(call_relay(far, o1)[0], "mem", near)
    own1, other1, kept1, inner_coef = call_interior(False, p, far, far_partner, near_counts, o1)
    own0, other0, kept0 = call_interior(True, p, near_g, partner, inner_coef, own1)
    e0 = lax.ppermute(e0, "strip", even)
    o0 = lax.ppermute(o0, "strip", odd)
    e1 = lax.ppermute(e1, "strip", even)
    o1 = lax.ppermute(o1, "strip", odd)
    eown0, eother0, edge_coef = call_edges(True, p, kept0, e0, o0, near_counts)
    eown1, eother1 = call_edges(False, p, kept1, e1, o1, edge_coef, eown0)

    inner = lax.ppermute(own1, "mem", across) + lax.ppermute(other1, "mem", cross)
    near0 = lax.ppermute(other0, "mem", near)
    enear0 = lax.ppermute(eother0, "mem", near)
    eown1, eother1 = call_relay(eown1, eother1, inner)
    efar1 = lax.ppermute(eown1, "mem", across)
    ecross1 = lax.ppermute(eother1, "mem", cross)
    return kernel_call(
        lambda *refs: finish(scale, *refs), shape(own, rows, ny), [], 1024, "finish"
    )(own0, near0, inner, eown0, enear0, efar1, ecross1)


def solution(mesh):
    return jax.shard_map(
        per_device,
        mesh=mesh,
        in_specs=(P("mem", "strip", None), P("mem", None, "strip", None), P("strip", None)),
        out_specs=P("mem", "strip", None),
        check_vma=False,
    )
```

```python
import functools
import math

import jax
import jax.numpy as jnp
from jax import lax
from jax.experimental import pallas as pl
from jax.experimental.pallas import tpu as pltpu
from jax.sharding import PartitionSpec as P

SLOTS = 2
VARS = 4
FIELDS = 8
SWEEPS = 4

COEFF_X = 0.35
COEFF_Y = 0.12
CENTRE = 1.0 - 2.0 * COEFF_X - 2.0 * COEFF_Y
RATIO = COEFF_Y / COEFF_X

LANES = 128
TILE = 8
HALF = 16
VMEM_BYTES = 40 * 2**20
PREPARE_FLOPS = 10**10
EDGE_GROUP = 8
INNER_GROUP = 2


def kernel_call(body, out_shape, scratch, flops, name, outside={}):
    def call(*args):
        spaces = [outside.get(i, pltpu.VMEM) for i in range(len(args))]
        return pl.pallas_call(
            body,
            out_shape=out_shape,
            in_specs=[pl.BlockSpec(memory_space=space) for space in spaces],
            out_specs=jax.tree.map(lambda _: pl.BlockSpec(memory_space=pltpu.VMEM), out_shape),
            scratch_shapes=scratch,
            compiler_params=pltpu.CompilerParams(vmem_limit_bytes=VMEM_BYTES),
            cost_estimate=pl.CostEstimate(flops=flops, bytes_accessed=1024, transcendentals=0),
            name=name,
        )(*args)

    return call


def lane_masks():
    lane = lax.broadcasted_iota(jnp.int32, (TILE, LANES), 1)
    return lane == 0, lane == LANES - 1


def top_half():
    return lax.broadcasted_iota(jnp.int32, (TILE, LANES), 0) < TILE // 2


def cols(j):
    return pl.ds(j * LANES, LANES)


def sides(values, first, last):
    zero = jnp.zeros_like(values[0])
    count = len(values)
    sums = []
    for j in range(count):
        left = jnp.where(last, values[j - 1] if j else zero, values[j])
        right = jnp.where(first, values[j + 1] if j + 1 < count else zero, values[j])
        sums.append(pltpu.roll(left, 1, 1) + pltpu.roll(right, LANES - 1, 1))
    return sums


def fields_of(local, own):
    shares = VARS // own
    mem = lax.axis_index("mem")
    slot, share = mem // shares, mem % shares
    slot = slot if local else SLOTS - 1 - slot
    return [slot * VARS + at * own + k for at in (share, shares - 1 - share) for k in range(own)]


def prepare(g_ref, counts_ref, near_g_ref, rim_ref, near_counts_ref, sem):
    rows = g_ref.shape[1]
    copies = [
        pltpu.make_async_copy(g_ref.at[:, 0:TILE], rim_ref.at[:, 0:TILE], sem.at[0]),
        pltpu.make_async_copy(g_ref.at[:, rows - TILE : rows], rim_ref.at[:, TILE : 2 * TILE], sem.at[1]),
        pltpu.make_async_copy(g_ref, near_g_ref, sem.at[2]),
        pltpu.make_async_copy(counts_ref, near_counts_ref, sem.at[3]),
    ]
    for copy in copies:
        copy.start()
    for copy in copies:
        copy.wait()


def weights_of(own, refs):
    return [(ref, k) for ref in refs for k in range(own)]


def project_edges(local, own, p_ref, *rest):
    if local:
        *g_refs, counts_ref, e_ref, o_ref, token_ref = rest
    else:
        *g_refs, _, e_ref, o_ref, token_ref = rest
    members, _, rows, ny = p_ref.shape
    even = lax.axis_index("strip") % 2 == 0
    half = top_half()
    fields = fields_of(local, own)
    grads = weights_of(own, g_refs)

    token_ref[...] = jnp.zeros_like(token_ref)

    def put(row, j, top, bottom):
        e_ref[row, :, cols(j)] = jnp.where(even, bottom, top)
        o_ref[row, :, cols(j)] = jnp.where(even, top, bottom)

    if local:
        for j in range(ny // LANES):
            top = counts_ref[0:TILE, cols(j)].astype(jnp.float32)
            bottom = counts_ref[rows - TILE : rows, cols(j)].astype(jnp.float32)
            put(members // 2, j, top, pltpu.roll(bottom, TILE // 2, 0))

    def pair(q):
        for j in range(ny // LANES):
            tops, bottoms = [], []
            for m in (2 * q, 2 * q + 1):
                top = bottom = None
                for f, (g_ref, k) in zip(fields, grads):
                    low = p_ref[m, f, 0:HALF, cols(j)].astype(jnp.float32)[0:TILE]
                    high = p_ref[m, f, rows - HALF : rows, cols(j)].astype(jnp.float32)[HALF - TILE :]
                    low = low * g_ref[k, 0:TILE, cols(j)]
                    high = high * g_ref[k, g_ref.shape[1] - TILE : g_ref.shape[1], cols(j)]
                    top = low if top is None else top + low
                    bottom = high if bottom is None else bottom + high
                tops.append(top)
                bottoms.append(bottom)
            top = jnp.where(half, tops[0], pltpu.roll(tops[1], TILE // 2, 0))
            bottom = jnp.where(half, pltpu.roll(bottoms[0], TILE // 2, 0), bottoms[1])
            put(q, j, top, bottom)

    pl.loop(0, members // 2)(pair)


def interior(local, begin, stage, p_ref, *refs):
    if stage == 0:
        *g_refs, counts_ref, _, own_ref, other_ref, kept_ref, coef, buf_a, buf_b, total_ref = refs
    elif stage == 1:
        *g_refs, coef, _, own_ref, other_ref, kept_ref, buf_a, buf_b, total_ref = refs
    else:
        g_refs, (coef, counts_ref, e_ref, o_ref), refs = refs[:2], refs[2:6], refs[6:]
        own_so_far, other_so_far, _, own_ref, other_ref, kept_ref, edge_coef, buf_a, buf_b, total_ref, halo = refs
        edge_weights(counts_ref, e_ref, o_ref, edge_coef, halo)
    members, _, rows, ny = p_ref.shape
    own = own_ref.shape[0]
    blocks = ny // LANES
    group = buf_a.shape[0]
    first, last = lane_masks()
    half = top_half()
    fields = fields_of(local, own)
    grads = weights_of(own, g_refs)
    sums = [(own_ref, k) for k in range(own)] + [(other_ref, k) for k in range(own)]
    skip = TILE // 2
    whole = list(range(0, rows, TILE))
    kept = list(range(skip, rows - skip, TILE))
    for t in range(1, 1 if stage else SWEEPS):
        for j in range(blocks):
            total_ref[0, j] = (counts_ref[:, cols(j)] > t).astype(jnp.float32)
            for n, r in enumerate(kept if t == SWEEPS - 1 else whole):
                active = total_ref[0, j, r : r + TILE]
                coef[t - 1, 0, j, n * TILE : (n + 1) * TILE] = active * COEFF_X
                coef[t - 1, 1, j, n * TILE : (n + 1) * TILE] = 1.0 - active * (1.0 - CENTRE)
    zero = jnp.zeros((TILE, LANES), jnp.float32)
    for buf in (buf_a, buf_b):
        for i in range(group):
            for j in range(blocks):
                buf[i, j, 0:TILE] = zero
                buf[i, j, TILE + rows :] = zero
    total_ref[...] = jnp.zeros_like(total_ref)

    def step(s, carry):
        base = begin + s * group
        for r in range(0, rows, HALF):
            for j in range(blocks):
                weights = [g_ref[k, r : r + HALF, cols(j)] for g_ref, k in grads]
                for i in range(group):
                    total = None
                    for f, w in zip(fields, weights):
                        term = p_ref[base + i, f, r : r + HALF, cols(j)].astype(jnp.float32) * w
                        total = term if total is None else total + term
                    buf_a[i, j, TILE + r : TILE + r + HALF] = total
        src, dst = buf_a, buf_b
        for t in range(SWEEPS):
            for i in range(group):
                for j in range(blocks):
                    low, high = TILE + t, rows - t
                    tile = jnp.where(half, src[i, j, low : low + TILE], src[i, j, high : high + TILE])
                    kept_ref[s * group + i, t * TILE : (t + 1) * TILE, cols(j)] = tile
            for n, r in enumerate(kept if t == SWEEPS - 1 else whole):
                at, to = TILE + r, TILE + n * TILE
                for i in range(group):
                    centre = [src[i, j, at : at + TILE] for j in range(blocks)]
                    lateral = sides(centre, first, last)
                    for j in range(blocks):
                        stacked = src[i, j, at - 1 : at - 1 + TILE] + src[i, j, at + 1 : at + 1 + TILE]
                        moved = stacked + RATIO * lateral[j]
                        if t == 0:
                            new = COEFF_X * moved + CENTRE * centre[j]
                        else:
                            own_row = pl.ds(n * TILE, TILE)
                            new = coef[t - 1, 0, j, own_row] * moved + coef[t - 1, 1, j, own_row] * centre[j]
                        dst[i, j, to : to + TILE] = new
            src, dst = dst, src
        for r in range(0, rows, HALF):
            for j in range(blocks):
                smooth = [src[i, j, TILE - skip + r : TILE - skip + r + HALF] for i in range(group)]
                for n, f in enumerate(fields):
                    total = total_ref[n, j, r : r + HALF]
                    for i in range(group):
                        total = total + p_ref[base + i, f, r : r + HALF, cols(j)].astype(jnp.float32) * smooth[i]
                    total_ref[n, j, r : r + HALF] = total
        return carry

    lax.fori_loop(0, kept_ref.shape[0] // group, step, 0)
    so_far = [(ref, k) for ref in (own_so_far, other_so_far) for k in range(own)] if stage == 2 else None
    for n, (ref, k) in enumerate(sums):
        for j in range(blocks):
            for r in range(0, rows - TILE, TILE):
                total = total_ref[n, j, skip + r : skip + r + TILE]
                if so_far:
                    total = total + so_far[n][0][k, r : r + TILE, cols(j)]
                ref[k, r : r + TILE, cols(j)] = total


def sent_tiles(e_ref, o_ref, q, j):
    even = lax.axis_index("strip") % 2 == 0
    e, o = e_ref[q, :, cols(j)], o_ref[q, :, cols(j)]
    return jnp.where(even, o, e), jnp.where(even, e, o)


def merged(ref, low, high):
    return jnp.where(top_half(), ref[low : low + TILE], ref[high : high + TILE])


def edge_weights(counts_ref, e_ref, o_ref, coef, halo):
    rows, ny = counts_ref.shape
    for j in range(ny // LANES):
        above, below = sent_tiles(e_ref, o_ref, e_ref.shape[0] - 1, j)
        halo[j, 4:12] = above
        halo[j, 24:32] = below
        halo[j, 8:16] = counts_ref[0:TILE, cols(j)].astype(jnp.float32)
        halo[j, 16:24] = counts_ref[rows - TILE : rows, cols(j)].astype(jnp.float32)
        for t in range(SWEEPS):
            active = (merged(halo.at[j], 5 + t, 19 - t) > t).astype(jnp.float32)
            coef[t, 0, j] = active * COEFF_X
            coef[t, 1, j] = 1.0 - active * (1.0 - CENTRE)


def edges(local, p_ref, *refs):
    *kept_refs, e_ref, o_ref, coef, _, own_ref, other_ref, win_a, win_b = refs
    members, _, rows, ny = p_ref.shape
    own = own_ref.shape[0]
    blocks = ny // LANES
    first, last = lane_masks()
    half = top_half()
    fields = fields_of(local, own)
    sums = [(own_ref, k) for k in range(own)] + [(other_ref, k) for k in range(own)]
    start = TILE

    own_ref[...] = jnp.zeros_like(own_ref)
    other_ref[...] = jnp.zeros_like(other_ref)

    group = win_a.shape[0]

    def step(begin, kept_ref, s, carry):
        base = begin + s * group
        for j in range(blocks):
            for i in range(0, group, 2):
                above, below = sent_tiles(e_ref, o_ref, base // 2 + i // 2, j)
                win_a[i, j, start : start + TILE] = above
                win_a[i, j, start + 12 : start + 20] = below
                win_a[i + 1, j, start - 4 : start + 4] = above
                win_a[i + 1, j, start + 8 : start + 16] = below
            for i in range(group):
                win_a[i, j, start + 4 : start + 12] = kept_ref[s * group + i, 0:TILE, cols(j)]
        src, dst = win_a, win_b
        smooth = [[] for i in range(group)]
        for t in range(SWEEPS):
            weights = [[coef[t, c, j] for j in range(blocks)] for c in range(2)]
            for i in range(group):
                centre = [merged(src.at[i, j], start + 1, start + 7) for j in range(blocks)]
                lateral = sides(centre, first, last)
                for j in range(blocks):
                    stacked = merged(src.at[i, j], start, start + 6) + merged(src.at[i, j], start + 2, start + 8)
                    new = weights[0][j] * (stacked + RATIO * lateral[j]) + weights[1][j] * centre[j]
                    if t == SWEEPS - 1:
                        smooth[i].append(new)
                    else:
                        dst[i, j, start : start + TILE] = new
                        dst[i, j, start + 8 : start + 16] = new
                        dst[i, j, start + 4 : start + 12] = kept_ref[s * group + i, (t + 1) * TILE : (t + 2) * TILE, cols(j)]
            src, dst = dst, src
        for j in range(blocks):
            for f, (ref, k) in zip(fields, sums):
                total = ref[k, :, cols(j)]
                for i in range(group):
                    low = p_ref[base + i, f, 0:HALF, cols(j)].astype(jnp.float32)[0:TILE]
                    high = p_ref[base + i, f, rows - HALF : rows, cols(j)].astype(jnp.float32)[HALF - TILE :]
                    total = total + jnp.where(half, low, high) * smooth[i][j]
                ref[k, :, cols(j)] = total
        return carry

    begin = 0
    for kept_ref in kept_refs:
        lax.fori_loop(0, kept_ref.shape[0] // group, functools.partial(step, begin, kept_ref), 0)
        begin += kept_ref.shape[0]


def relay(*refs):
    count = len(refs) // 2
    for ref, out_ref in zip(refs[:count], refs[count + 1 :]):
        out_ref[...] = ref[...]


def gather_up(own_ref, near_ref, inner_ref, *refs):
    *edge_refs, out_ref = refs
    own, rows, ny = out_ref.shape
    half = top_half()
    for k in range(own):
        for j in range(ny // LANES):
            edge = sum(ref[k, :, cols(j)] for ref in edge_refs[1:]) + edge_refs[0][k, :, cols(j)]
            parts = [edge]
            for r in range(0, rows - TILE, TILE):
                inner = own_ref[k, r : r + TILE, cols(j)] + near_ref[k, r : r + TILE, cols(j)] + inner_ref[k, r : r + TILE, cols(j)]
                parts.append(pltpu.roll(inner, TILE // 2, 0))
            parts.append(edge)
            for n in range(rows // TILE):
                out_ref[k, n * TILE : (n + 1) * TILE, cols(j)] = jnp.where(half, parts[n], parts[n + 1])


def finish(scale, sum_ref, edge_ref, out_ref):
    own, rows, ny = out_ref.shape
    half = top_half()
    for k in range(own):
        for j in range(ny // LANES):
            edge = edge_ref[k, :, cols(j)]
            none = jnp.zeros_like(edge)
            out_ref[k, 0:TILE, cols(j)] = (sum_ref[k, 0:TILE, cols(j)] + jnp.where(half, edge, none)) * scale
            middle = pl.ds(TILE, rows - 2 * TILE)
            out_ref[k, middle, cols(j)] = sum_ref[k, middle, cols(j)] * scale
            end = pl.ds(rows - TILE, TILE)
            out_ref[k, end, cols(j)] = (sum_ref[k, end, cols(j)] + jnp.where(half, none, edge)) * scale


def per_device(gradient, perturbations, counts):
    members, _, rows, ny = perturbations.shape
    own = gradient.shape[0]
    mem, strips = lax.axis_size("mem"), lax.axis_size("strip")
    shares = VARS // own
    blocks = ny // LANES
    assert shares == 2 and mem == shares * SLOTS and members % 2 == 0
    scale = 1.0 / math.sqrt(members * mem * FIELDS)
    f32 = jnp.float32

    near = [(i, i ^ 1) for i in range(mem)]
    across = [(i, (i + shares) % mem) for i in range(mem)]
    cross = [(i, (i + shares) % mem ^ 1) for i in range(mem)]
    even = [(i, i ^ 1) for i in range(strips) if i ^ 1 < strips]
    odd = [(i, i + 1) for i in range(1, strips - 1, 2)]
    odd = odd + [(j, i) for i, j in odd]

    def shape(*dims):
        return jax.ShapeDtypeStruct(dims, f32)

    def window(*lead):
        return pltpu.VMEM((*lead, blocks, 4 * TILE, LANES), f32)

    def call_prepare(*args):
        outs = (shape(own, rows, ny), shape(own, 2 * TILE, ny), jax.ShapeDtypeStruct((rows, ny), counts.dtype))
        stored = [pltpu.with_memory_space_constraint(x, pltpu.HBM) for x in args]
        outside = {0: pl.ANY, 1: pl.ANY}
        return kernel_call(prepare, outs, [pltpu.SemaphoreType.DMA((4,))], PREPARE_FLOPS, "prepare", outside)(*stored)

    def call_project(local, *args):
        pairs = members // 2 + (1 if local else 0)
        outs = (shape(pairs, TILE, ny), shape(pairs, TILE, ny), shape(TILE, LANES))
        outside = {} if local else {len(args) - 1: pl.ANY}
        body = lambda *refs: project_edges(local, own, *refs)
        return kernel_call(body, outs, [], 1024, "project", outside=outside)(*args)

    def call_relay(*args):
        outs = tuple(shape(*x.shape) for x in args[:-1])
        return kernel_call(relay, outs, [], 1024, "relay", outside={len(outs): pl.ANY})(*args)

    def call_interior(local, begin, count, stage, *args):
        total = pltpu.VMEM((VARS, blocks, rows, LANES), f32)
        buf = pltpu.VMEM((INNER_GROUP, blocks, rows + 2 * TILE, LANES), f32)
        outs = (shape(own, rows - TILE, ny), shape(own, rows - TILE, ny), shape(count, SWEEPS * TILE, ny))
        outs += ((shape(SWEEPS - 1, 2, blocks, rows, LANES),), (), (shape(SWEEPS, 2, blocks, TILE, LANES),))[stage]
        scratch = [buf, buf, total] + ([window()] if stage == 2 else [])
        body = lambda *refs: interior(local, begin, stage, *refs)
        return kernel_call(body, outs, scratch, 1024, "interior", outside={len(args) - 1: pl.ANY})(*args)

    def call_edges(local, *args):
        outs = (shape(own, TILE, ny), shape(own, TILE, ny))
        body = lambda *refs: edges(local, *refs)
        scratch = [window(EDGE_GROUP), window(EDGE_GROUP)]
        return kernel_call(body, outs, scratch, 1024, "edges", outside={len(args) - 1: pl.ANY})(*args)

    near_g, rim, near_counts = call_prepare(gradient, counts)
    partner = lax.ppermute(gradient, "mem", near)
    far = lax.ppermute(gradient, "mem", across)
    far_rim = lax.ppermute(rim, "mem", cross)

    p = perturbations
    part = members // 2
    e0, o0, token0 = call_project(True, p, near_g, partner, near_counts)
    own0, other0, kept0, inner_coef = call_interior(True, 0, part, 0, p, near_g, partner, near_counts, token0)
    e0 = lax.ppermute(e0, "strip", even)
    o0 = lax.ppermute(o0, "strip", odd)
    e1, o1, token1 = call_project(False, p, far, far_rim, own0)
    far_partner = lax.ppermute(call_relay(far, token1)[0], "mem", near)
    own1, other1, kept1 = call_interior(False, 0, members, 1, p, far, far_partner, inner_coef, token1)
    e1 = lax.ppermute(e1, "strip", even)
    o1 = lax.ppermute(o1, "strip", odd)
    own0, other0, kept2, edge_coef = call_interior(
        True, part, part, 2, p, near_g, partner, inner_coef, near_counts, e0, o0, own0, other0, own1
    )
    eown1, eother1 = call_edges(False, p, kept1, e1, o1, edge_coef, own0)
    eown0, eother0 = call_edges(True, p, kept0, kept2, e0, o0, edge_coef, eown1)

    inner = lax.ppermute(own1, "mem", across) + lax.ppermute(other1, "mem", cross)
    near0 = lax.ppermute(other0, "mem", near)
    eown1, eother1 = call_relay(eown1, eother1, inner)
    efar1 = lax.ppermute(eown1, "mem", across)
    ecross1 = lax.ppermute(eother1, "mem", cross)
    enear0 = lax.ppermute(eother0, "mem", near)
    total = kernel_call(gather_up, shape(own, rows, ny), [], PREPARE_FLOPS, "gather_up")(
        own0, near0, inner, eown0, efar1, ecross1
    )
    return kernel_call(
        lambda *refs: finish(scale, *refs), shape(own, rows, ny), [], 1024, "finish"
    )(total, enear0)


def solution(mesh):
    return jax.shard_map(
        per_device,
        mesh=mesh,
        in_specs=(P("mem", "strip", None), P("mem", None, "strip", None), P("strip", None)),
        out_specs=P("mem", "strip", None),
        check_vma=False,
    )
```

```python
import functools
import math

import jax
import jax.numpy as jnp
from jax import lax
from jax.experimental import pallas as pl
from jax.experimental.pallas import tpu as pltpu
from jax.sharding import PartitionSpec as P

SLOTS = 2
VARS = 4
FIELDS = 8
SWEEPS = 4

COEFF_X = 0.35
COEFF_Y = 0.12
CENTRE = 1.0 - 2.0 * COEFF_X - 2.0 * COEFF_Y
RATIO = COEFF_Y / COEFF_X

LANES = 128
TILE = 8
HALF = 16
VMEM_BYTES = 40 * 2**20
PREPARE_FLOPS = 10**10
EDGE_GROUP = 8
INNER_GROUP = 2


def kernel_call(body, out_shape, scratch, flops, name, outside={}):
    def call(*args):
        spaces = [outside.get(i, pltpu.VMEM) for i in range(len(args))]
        return pl.pallas_call(
            body,
            out_shape=out_shape,
            in_specs=[pl.BlockSpec(memory_space=space) for space in spaces],
            out_specs=jax.tree.map(lambda _: pl.BlockSpec(memory_space=pltpu.VMEM), out_shape),
            scratch_shapes=scratch,
            compiler_params=pltpu.CompilerParams(vmem_limit_bytes=VMEM_BYTES),
            cost_estimate=pl.CostEstimate(flops=flops, bytes_accessed=1024, transcendentals=0),
            name=name,
        )(*args)

    return call


def lane_masks():
    lane = lax.broadcasted_iota(jnp.int32, (TILE, LANES), 1)
    return lane == 0, lane == LANES - 1


def top_half():
    return lax.broadcasted_iota(jnp.int32, (TILE, LANES), 0) < TILE // 2


def cols(j):
    return pl.ds(j * LANES, LANES)


def sides(values, first, last):
    zero = jnp.zeros_like(values[0])
    count = len(values)
    sums = []
    for j in range(count):
        left = jnp.where(last, values[j - 1] if j else zero, values[j])
        right = jnp.where(first, values[j + 1] if j + 1 < count else zero, values[j])
        sums.append(pltpu.roll(left, 1, 1) + pltpu.roll(right, LANES - 1, 1))
    return sums


def fields_of(local, own):
    shares = VARS // own
    mem = lax.axis_index("mem")
    slot, share = mem // shares, mem % shares
    slot = slot if local else SLOTS - 1 - slot
    return [slot * VARS + at * own + k for at in (share, shares - 1 - share) for k in range(own)]


def prepare(g_ref, counts_ref, near_g_ref, rim_ref, middle_ref, near_counts_ref, sem):
    rows = g_ref.shape[1]
    copies = [
        pltpu.make_async_copy(g_ref.at[:, 0:TILE], rim_ref.at[:, 0:TILE], sem.at[0]),
        pltpu.make_async_copy(g_ref.at[:, rows - TILE : rows], rim_ref.at[:, TILE : 2 * TILE], sem.at[1]),
        pltpu.make_async_copy(g_ref, near_g_ref, sem.at[2]),
        pltpu.make_async_copy(counts_ref, near_counts_ref, sem.at[3]),
        pltpu.make_async_copy(g_ref.at[:, TILE : rows - TILE], middle_ref, sem.at[4]),
    ]
    for copy in copies:
        copy.start()
    for copy in copies:
        copy.wait()


def weights_of(own, refs):
    return [(ref, k) for ref in refs for k in range(own)]


def project_edges(local, own, p_ref, *rest):
    if local:
        *g_refs, counts_ref, e_ref, o_ref, token_ref = rest
    else:
        *g_refs, _, e_ref, o_ref, token_ref = rest
    members, _, rows, ny = p_ref.shape
    even = lax.axis_index("strip") % 2 == 0
    half = top_half()
    fields = fields_of(local, own)
    grads = weights_of(own, g_refs)

    token_ref[...] = jnp.zeros_like(token_ref)

    def put(row, j, top, bottom):
        e_ref[row, :, cols(j)] = jnp.where(even, bottom, top)
        o_ref[row, :, cols(j)] = jnp.where(even, top, bottom)

    if local:
        for j in range(ny // LANES):
            top = counts_ref[0:TILE, cols(j)].astype(jnp.float32)
            bottom = counts_ref[rows - TILE : rows, cols(j)].astype(jnp.float32)
            put(members // 2, j, top, pltpu.roll(bottom, TILE // 2, 0))

    def pair(q):
        for j in range(ny // LANES):
            tops, bottoms = [], []
            for m in (2 * q, 2 * q + 1):
                top = bottom = None
                for f, (g_ref, k) in zip(fields, grads):
                    low = p_ref[m, f, 0:HALF, cols(j)].astype(jnp.float32)[0:TILE]
                    high = p_ref[m, f, rows - HALF : rows, cols(j)].astype(jnp.float32)[HALF - TILE :]
                    low = low * g_ref[k, 0:TILE, cols(j)]
                    high = high * g_ref[k, g_ref.shape[1] - TILE : g_ref.shape[1], cols(j)]
                    top = low if top is None else top + low
                    bottom = high if bottom is None else bottom + high
                tops.append(top)
                bottoms.append(bottom)
            top = jnp.where(half, tops[0], pltpu.roll(tops[1], TILE // 2, 0))
            bottom = jnp.where(half, pltpu.roll(bottoms[0], TILE // 2, 0), bottoms[1])
            put(q, j, top, bottom)

    pl.loop(0, members // 2)(pair)


def interior(local, begin, stage, p_ref, *refs):
    if stage == 0:
        *g_refs, counts_ref, _, own_ref, other_ref, kept_ref, coef, buf_a, buf_b, total_ref = refs
    elif stage == 1:
        *g_refs, coef, _, own_ref, other_ref, kept_ref, buf_a, buf_b, total_ref = refs
    else:
        g_refs, (coef, counts_ref, e_ref, o_ref), refs = refs[:2], refs[2:6], refs[6:]
        own_so_far, other_so_far, _, own_ref, other_ref, kept_ref, edge_coef, buf_a, buf_b, total_ref, halo = refs
        edge_weights(counts_ref, e_ref, o_ref, edge_coef, halo)
    members, _, rows, ny = p_ref.shape
    own = own_ref.shape[0]
    blocks = ny // LANES
    group = buf_a.shape[0]
    first, last = lane_masks()
    half = top_half()
    fields = fields_of(local, own)
    grads = weights_of(own, g_refs)
    sums = [(own_ref, k) for k in range(own)] + [(other_ref, k) for k in range(own)]
    skip = TILE // 2
    whole = list(range(0, rows, TILE))
    kept = list(range(skip, rows - skip, TILE))
    for t in range(1, 1 if stage else SWEEPS):
        for j in range(blocks):
            total_ref[0, j] = (counts_ref[:, cols(j)] > t).astype(jnp.float32)
            for n, r in enumerate(kept if t == SWEEPS - 1 else whole):
                active = total_ref[0, j, r : r + TILE]
                coef[t - 1, 0, j, n * TILE : (n + 1) * TILE] = active * COEFF_X
                coef[t - 1, 1, j, n * TILE : (n + 1) * TILE] = 1.0 - active * (1.0 - CENTRE)
    zero = jnp.zeros((TILE, LANES), jnp.float32)
    for buf in (buf_a, buf_b):
        for i in range(group):
            for j in range(blocks):
                buf[i, j, 0:TILE] = zero
                buf[i, j, TILE + rows :] = zero
    total_ref[...] = jnp.zeros_like(total_ref)

    def step(s, carry):
        base = begin + s * group
        for r in range(0, rows, HALF):
            for j in range(blocks):
                weights = [g_ref[k, r : r + HALF, cols(j)] for g_ref, k in grads]
                for i in range(group):
                    total = None
                    for f, w in zip(fields, weights):
                        term = p_ref[base + i, f, r : r + HALF, cols(j)].astype(jnp.float32) * w
                        total = term if total is None else total + term
                    buf_a[i, j, TILE + r : TILE + r + HALF] = total
        src, dst = buf_a, buf_b
        for t in range(SWEEPS):
            for i in range(group):
                for j in range(blocks):
                    low, high = TILE + t, rows - t
                    tile = jnp.where(half, src[i, j, low : low + TILE], src[i, j, high : high + TILE])
                    kept_ref[s * group + i, t * TILE : (t + 1) * TILE, cols(j)] = tile
            for n, r in enumerate(kept if t == SWEEPS - 1 else whole):
                at, to = TILE + r, TILE + n * TILE
                for i in range(group):
                    centre = [src[i, j, at : at + TILE] for j in range(blocks)]
                    lateral = sides(centre, first, last)
                    for j in range(blocks):
                        stacked = src[i, j, at - 1 : at - 1 + TILE] + src[i, j, at + 1 : at + 1 + TILE]
                        moved = stacked + RATIO * lateral[j]
                        if t == 0:
                            new = COEFF_X * moved + CENTRE * centre[j]
                        else:
                            own_row = pl.ds(n * TILE, TILE)
                            new = coef[t - 1, 0, j, own_row] * moved + coef[t - 1, 1, j, own_row] * centre[j]
                        dst[i, j, to : to + TILE] = new
            src, dst = dst, src
        for r in range(0, rows, HALF):
            for j in range(blocks):
                smooth = [src[i, j, TILE - skip + r : TILE - skip + r + HALF] for i in range(group)]
                for n, f in enumerate(fields):
                    total = total_ref[n, j, r : r + HALF]
                    for i in range(group):
                        total = total + p_ref[base + i, f, r : r + HALF, cols(j)].astype(jnp.float32) * smooth[i]
                    total_ref[n, j, r : r + HALF] = total
        return carry

    lax.fori_loop(0, kept_ref.shape[0] // group, step, 0)
    so_far = [(ref, k) for ref in (own_so_far, other_so_far) for k in range(own)] if stage == 2 else None
    for n, (ref, k) in enumerate(sums):
        for j in range(blocks):
            for r in range(0, rows - TILE, TILE):
                total = total_ref[n, j, skip + r : skip + r + TILE]
                if so_far:
                    total = total + so_far[n][0][k, r : r + TILE, cols(j)]
                ref[k, r : r + TILE, cols(j)] = total


def sent_tiles(e_ref, o_ref, q, j):
    even = lax.axis_index("strip") % 2 == 0
    e, o = e_ref[q, :, cols(j)], o_ref[q, :, cols(j)]
    return jnp.where(even, o, e), jnp.where(even, e, o)


def merged(ref, low, high):
    return jnp.where(top_half(), ref[low : low + TILE], ref[high : high + TILE])


def edge_weights(counts_ref, e_ref, o_ref, coef, halo):
    rows, ny = counts_ref.shape
    for j in range(ny // LANES):
        above, below = sent_tiles(e_ref, o_ref, e_ref.shape[0] - 1, j)
        halo[j, 4:12] = above
        halo[j, 24:32] = below
        halo[j, 8:16] = counts_ref[0:TILE, cols(j)].astype(jnp.float32)
        halo[j, 16:24] = counts_ref[rows - TILE : rows, cols(j)].astype(jnp.float32)
        for t in range(SWEEPS):
            active = (merged(halo.at[j], 5 + t, 19 - t) > t).astype(jnp.float32)
            coef[t, 0, j] = active * COEFF_X
            coef[t, 1, j] = 1.0 - active * (1.0 - CENTRE)


def edges(local, p_ref, *refs):
    *kept_refs, e_ref, o_ref, coef, _, own_ref, other_ref, win_a, win_b = refs
    members, _, rows, ny = p_ref.shape
    own = own_ref.shape[0]
    blocks = ny // LANES
    first, last = lane_masks()
    half = top_half()
    fields = fields_of(local, own)
    sums = [(own_ref, k) for k in range(own)] + [(other_ref, k) for k in range(own)]
    start = TILE

    own_ref[...] = jnp.zeros_like(own_ref)
    other_ref[...] = jnp.zeros_like(other_ref)

    group = win_a.shape[0]

    def step(begin, kept_ref, s, carry):
        base = begin + s * group
        for j in range(blocks):
            for i in range(0, group, 2):
                above, below = sent_tiles(e_ref, o_ref, base // 2 + i // 2, j)
                win_a[i, j, start : start + TILE] = above
                win_a[i, j, start + 12 : start + 20] = below
                win_a[i + 1, j, start - 4 : start + 4] = above
                win_a[i + 1, j, start + 8 : start + 16] = below
            for i in range(group):
                win_a[i, j, start + 4 : start + 12] = kept_ref[s * group + i, 0:TILE, cols(j)]
        src, dst = win_a, win_b
        smooth = [[] for i in range(group)]
        for t in range(SWEEPS):
            weights = [[coef[t, c, j] for j in range(blocks)] for c in range(2)]
            for i in range(group):
                centre = [merged(src.at[i, j], start + 1, start + 7) for j in range(blocks)]
                lateral = sides(centre, first, last)
                for j in range(blocks):
                    stacked = merged(src.at[i, j], start, start + 6) + merged(src.at[i, j], start + 2, start + 8)
                    new = weights[0][j] * (stacked + RATIO * lateral[j]) + weights[1][j] * centre[j]
                    if t == SWEEPS - 1:
                        smooth[i].append(new)
                    else:
                        dst[i, j, start : start + TILE] = new
                        dst[i, j, start + 8 : start + 16] = new
                        dst[i, j, start + 4 : start + 12] = kept_ref[s * group + i, (t + 1) * TILE : (t + 2) * TILE, cols(j)]
            src, dst = dst, src
        for j in range(blocks):
            for f, (ref, k) in zip(fields, sums):
                total = ref[k, :, cols(j)]
                for i in range(group):
                    low = p_ref[base + i, f, 0:HALF, cols(j)].astype(jnp.float32)[0:TILE]
                    high = p_ref[base + i, f, rows - HALF : rows, cols(j)].astype(jnp.float32)[HALF - TILE :]
                    total = total + jnp.where(half, low, high) * smooth[i][j]
                ref[k, :, cols(j)] = total
        return carry

    begin = 0
    for kept_ref in kept_refs:
        lax.fori_loop(0, kept_ref.shape[0] // group, functools.partial(step, begin, kept_ref), 0)
        begin += kept_ref.shape[0]


def join(rim_ref, middle_ref, _, out_ref):
    rows = out_ref.shape[1]
    out_ref[:, 0:TILE] = rim_ref[:, 0:TILE]
    out_ref[:, TILE : rows - TILE] = middle_ref[...]
    out_ref[:, rows - TILE : rows] = rim_ref[:, TILE : 2 * TILE]


def gather_up(own_ref, near_ref, inner_ref, *refs):
    *edge_refs, out_ref = refs
    own, rows, ny = out_ref.shape
    half = top_half()
    for k in range(own):
        for j in range(ny // LANES):
            edge = sum(ref[k, :, cols(j)] for ref in edge_refs[1:]) + edge_refs[0][k, :, cols(j)]
            parts = [edge]
            for r in range(0, rows - TILE, TILE):
                inner = own_ref[k, r : r + TILE, cols(j)] + near_ref[k, r : r + TILE, cols(j)] + inner_ref[k, r : r + TILE, cols(j)]
                parts.append(pltpu.roll(inner, TILE // 2, 0))
            parts.append(edge)
            for n in range(rows // TILE):
                out_ref[k, n * TILE : (n + 1) * TILE, cols(j)] = jnp.where(half, parts[n], parts[n + 1])


def finish(scale, sum_ref, edge_ref, out_ref):
    own, rows, ny = out_ref.shape
    half = top_half()
    for k in range(own):
        for j in range(ny // LANES):
            edge = edge_ref[k, :, cols(j)]
            none = jnp.zeros_like(edge)
            out_ref[k, 0:TILE, cols(j)] = (sum_ref[k, 0:TILE, cols(j)] + jnp.where(half, edge, none)) * scale
            middle = pl.ds(TILE, rows - 2 * TILE)
            out_ref[k, middle, cols(j)] = sum_ref[k, middle, cols(j)] * scale
            end = pl.ds(rows - TILE, TILE)
            out_ref[k, end, cols(j)] = (sum_ref[k, end, cols(j)] + jnp.where(half, none, edge)) * scale


def per_device(gradient, perturbations, counts):
    members, _, rows, ny = perturbations.shape
    own = gradient.shape[0]
    mem, strips = lax.axis_size("mem"), lax.axis_size("strip")
    shares = VARS // own
    blocks = ny // LANES
    assert shares == 2 and mem == shares * SLOTS and members % 2 == 0
    scale = 1.0 / math.sqrt(members * mem * FIELDS)
    f32 = jnp.float32

    near = [(i, i ^ 1) for i in range(mem)]
    across = [(i, (i + shares) % mem) for i in range(mem)]
    cross = [(i, (i + shares) % mem ^ 1) for i in range(mem)]
    even = [(i, i ^ 1) for i in range(strips) if i ^ 1 < strips]
    odd = [(i, i + 1) for i in range(1, strips - 1, 2)]
    odd = odd + [(j, i) for i, j in odd]

    def shape(*dims):
        return jax.ShapeDtypeStruct(dims, f32)

    def window(*lead):
        return pltpu.VMEM((*lead, blocks, 4 * TILE, LANES), f32)

    def call_prepare(*args):
        outs = (shape(own, rows, ny), shape(own, 2 * TILE, ny), shape(own, rows - 2 * TILE, ny))
        outs += (jax.ShapeDtypeStruct((rows, ny), counts.dtype),)
        stored = [pltpu.with_memory_space_constraint(x, pltpu.HBM) for x in args]
        outside = {0: pl.ANY, 1: pl.ANY}
        return kernel_call(prepare, outs, [pltpu.SemaphoreType.DMA((5,))], PREPARE_FLOPS, "prepare", outside)(*stored)

    def call_project(local, *args):
        pairs = members // 2 + (1 if local else 0)
        outs = (shape(pairs, TILE, ny), shape(pairs, TILE, ny), shape(TILE, LANES))
        outside = {} if local else {len(args) - 1: pl.ANY}
        body = lambda *refs: project_edges(local, own, *refs)
        return kernel_call(body, outs, [], 1024, "project", outside=outside)(*args)

    def call_interior(local, begin, count, stage, *args):
        total = pltpu.VMEM((VARS, blocks, rows, LANES), f32)
        buf = pltpu.VMEM((INNER_GROUP, blocks, rows + 2 * TILE, LANES), f32)
        outs = (shape(own, rows - TILE, ny), shape(own, rows - TILE, ny), shape(count, SWEEPS * TILE, ny))
        outs += ((shape(SWEEPS - 1, 2, blocks, rows, LANES),), (), (shape(SWEEPS, 2, blocks, TILE, LANES),))[stage]
        scratch = [buf, buf, total] + ([window()] if stage == 2 else [])
        body = lambda *refs: interior(local, begin, stage, *refs)
        return kernel_call(body, outs, scratch, 1024, "interior", outside={len(args) - 1: pl.ANY})(*args)

    def call_edges(local, *args):
        outs = (shape(own, TILE, ny), shape(own, TILE, ny))
        body = lambda *refs: edges(local, *refs)
        scratch = [window(EDGE_GROUP), window(EDGE_GROUP)]
        return kernel_call(body, outs, scratch, 1024, "edges", outside={len(args) - 1: pl.ANY})(*args)

    near_g, rim, middle, near_counts = call_prepare(gradient, counts)
    partner = lax.ppermute(gradient, "mem", near)
    far = lax.ppermute(gradient, "mem", across)
    far_rim = lax.ppermute(rim, "mem", cross)
    far_middle = lax.ppermute(middle, "mem", cross)

    p = perturbations
    part = members // 2
    e0, o0, token0 = call_project(True, p, near_g, partner, near_counts)
    own0, other0, kept0, inner_coef = call_interior(True, 0, part, 0, p, near_g, partner, near_counts, token0)
    e0 = lax.ppermute(e0, "strip", even)
    o0 = lax.ppermute(o0, "strip", odd)
    e1, o1, token1 = call_project(False, p, far, far_rim, own0)
    far_partner = kernel_call(join, shape(own, rows, ny), [], 1024, "join", outside={2: pl.ANY})(
        far_rim, far_middle, token1
    )
    own1, other1, kept1 = call_interior(False, 0, members, 1, p, far, far_partner, inner_coef, token1)
    e1 = lax.ppermute(e1, "strip", even)
    o1 = lax.ppermute(o1, "strip", odd)
    own0, other0, kept2, edge_coef = call_interior(
        True, part, part, 2, p, near_g, partner, inner_coef, near_counts, e0, o0, own0, other0, own1
    )
    eown1, eother1 = call_edges(False, p, kept1, e1, o1, edge_coef, own0)
    eown0, eother0 = call_edges(True, p, kept0, kept2, e0, o0, edge_coef, eown1)

    far1, cross1 = lax.ppermute(own1, "mem", across), lax.ppermute(other1, "mem", cross)
    near0 = lax.ppermute(other0, "mem", near)
    efar1 = lax.ppermute(eown1, "mem", across)
    ecross1 = lax.ppermute(eother1, "mem", cross)
    enear0 = lax.ppermute(eother0, "mem", near)
    total = kernel_call(gather_up, shape(own, rows, ny), [], PREPARE_FLOPS, "gather_up")(
        own0, near0, far1 + cross1, eown0, efar1, ecross1
    )
    return kernel_call(
        lambda *refs: finish(scale, *refs), shape(own, rows, ny), [], 1024, "finish"
    )(total, enear0)


def solution(mesh):
    return jax.shard_map(
        per_device,
        mesh=mesh,
        in_specs=(P("mem", "strip", None), P("mem", None, "strip", None), P("strip", None)),
        out_specs=P("mem", "strip", None),
        check_vma=False,
    )
```
